32 devices in a mesh: space: 8 (over z, y), member: 4 (over x, core).
Axes of the slice: x: 2, y: 2, z: 4, core: 2. Of those that a mesh axis runs over, the one named last changes fastest.
Arguments:
- start_temp: float32 [4, 16, 512, 128], P('member', None, 'space'), may hold values from -6 to 6
- cotangent: float32 [4, 16, 512, 128], P('member', None, 'space'), may hold values from -6 to 6
- conductivity: float32 [16, 512, 128], P(None, 'space'), may hold values from 1 to 4
- porosity: float32 [16, 512, 128], P(None, 'space'), may hold values from 0.02 to 0.3
- surface_temp: float32 [4, 512, 128], P('member', 'space'), may hold values from -8 to 8
- surface_offset: float32 [512, 128], P('space'), may hold values from -6 to 6
- basal_flux: float32 [512, 128], P('space'), may hold values from 1 to 6
- thickness: float32 [512, 128], P('space'), may hold values from 0.7 to 1.4
- tile_len: int32 [8], P('space'), may hold values from 1 to 64, 384 in all
Outputs:
- heated: float32 [4, 16, 512, 128], P('member', None, 'space')
- adj_temp: float32 [4, 16, 512, 128], P('member', None, 'space')
- new_cond: float32 [16, 512, 128], P(None, 'space')
- grad_offset: float32 [512, 128], P('space')
The draws below stay inside these ranges and needn't reach their ends.
Inputs may be any that keep to these rules, and one draw needn't show every extreme that they name: `tile_len`: the largest tile has exactly 64 live rows, and all tiles together hold 384 live rows.
All inputs are finite; a program needn't handle non-finite values. No bound on the sum of `tile_len` on one device may be relied on, other than what follows from the above.
Results may differ from the reference program's by a relative error of at most 0.00002.
Values sent between devices are 32-bit elements; how exact they have to be, the bound alone decides.
A program may use at most 64 MiB of HBM per device.

```python
import math
import jax
import jax.numpy as jnp
import numpy as np
from jax import lax

LAYERS = 16
TILE_ROWS = 64
ACROSS = 128
ROWS = 512
MEMBERS = 4
N_SPACE = 8


def levels(rng, dims, shards, least, largest):
    def one(dim, shards_of):
        steps = jax.random.uniform(jax.random.fold_in(jax.random.fold_in(rng, 6), dim), (shards_of,), jnp.float32, least / len(shards), largest / len(shards))
        return jnp.repeat(jnp.exp(steps), dims[dim] // shards_of).reshape((-1,) + (1,) * (len(dims) - dim - 1))

    factor_of = one(*shards[0])
    for cut in shards[1:]:
        factor_of = factor_of * one(*cut)
    return factor_of


def split_up(amount, total, most, lean):
    loads = [(1 << 20) // math.isqrt(rank ** lean) + 1 for rank in range(2, amount + 1)]
    spare, holding = total - most - (amount - 1), [1] * (amount - 1)
    while spare > 0:
        free = [i for i in range(amount - 1) if holding[i] < most]
        pool, budget = sum([loads[i] for i in free]), spare
        for i in free:
            extra = min(most - holding[i], max(1, budget * loads[i] // pool), spare)
            holding[i] = holding[i] + extra
            spare = spare - extra
    return np.array([most] + holding)


def uneven(own_key, count, total, bound, lean):
    if count == 2:
        one = jax.random.randint(own_key, (), max(1, total - bound), min(bound, total - 1) + 1)
        return jnp.stack([one, total - one])
    lengths = jnp.asarray(split_up(count, total, bound, lean), jnp.int32)
    couples = (count - 1) // 2
    donor, receiver = lengths[1:1 + 2 * couples:2], lengths[2:2 + 2 * couples:2]
    slack = jnp.minimum(donor - 1, bound - receiver)
    shifted = jax.random.randint(jax.random.fold_in(own_key, 1), (couples,), 0, 1 << 20) % (slack + 1)
    lengths = lengths.at[1:1 + 2 * couples:2].set(donor - shifted).at[2:2 + 2 * couples:2].set(receiver + shifted)
    return lengths[jax.random.permutation(jax.random.fold_in(own_key, 2), count)]


def noise(rng, dims, deviation, bound, shards=(), kind=jnp.bfloat16):
    drawn = deviation * jax.random.normal(rng, dims, jnp.float32)
    if shards:
        drawn = drawn * levels(rng, dims, shards, -0.22, 0.18)
    return jnp.clip(drawn, -bound, bound).astype(kind)


def setup_inputs(seed: int = 0) -> dict:
    key_of = jax.random.split(jax.random.key(seed), 10)
    return {
        "start_temp": noise(key_of[0], (MEMBERS, LAYERS, ROWS, ACROSS), 1.5, 6.0, ((0, 4), (2, 8)), jnp.float32),
        "cotangent": noise(key_of[1], (MEMBERS, LAYERS, ROWS, ACROSS), 1.0, 6.0, ((0, 4), (2, 8)), jnp.float32),
        "conductivity": jnp.clip(jnp.exp(math.log(4.0) - 1.3862944 * jax.random.uniform(key_of[2], (LAYERS, ROWS, ACROSS), jnp.float32) ** levels(key_of[2], (LAYERS, ROWS, ACROSS), ((1, 8),), -0.2, 0.2)), 1.0, 4.0),
        "porosity": jnp.clip(jnp.exp(math.log(0.3) - 2.7080503 * jax.random.uniform(key_of[3], (LAYERS, ROWS, ACROSS), jnp.float32) ** levels(key_of[3], (LAYERS, ROWS, ACROSS), ((1, 8),), -0.2, 0.2)), 0.02, 0.3),
        "surface_temp": noise(key_of[4], (MEMBERS, ROWS, ACROSS), 2.0, 8.0, ((0, 4), (1, 8)), jnp.float32),
        "surface_offset": noise(key_of[5], (ROWS, ACROSS), 1.0, 6.0, ((0, 8),), jnp.float32),
        "basal_flux": jnp.clip(1.0 + 5.0 * jax.random.uniform(key_of[6], (ROWS, ACROSS), jnp.float32) ** levels(key_of[6], (ROWS, ACROSS), ((0, 8),), -0.2, 0.2), 1.0, 6.0),
        "thickness": jnp.clip(0.7 + 0.7 * jax.random.uniform(key_of[7], (ROWS, ACROSS), jnp.float32) ** levels(key_of[7], (ROWS, ACROSS), ((0, 8),), -0.2, 0.2), 0.7, 1.4),
        "tile_len": uneven(key_of[8], N_SPACE, 3 * ROWS // 4, TILE_ROWS, 2).astype(jnp.int32),
    }


WIDTH_T = 0.5
LATENT = 16.0
STEP = 0.03
RATE = 0.5

def along_ridge(field, tile_len):
    layers = field.shape[0]
    across = field.shape[2]
    tiles = field.reshape(layers, N_SPACE, TILE_ROWS, across)
    last_index = (tile_len - 1).astype(jnp.int32)
    index = jnp.broadcast_to(last_index[None, :, None, None], (layers, N_SPACE, 1, across))
    last_rows = jnp.take_along_axis(tiles, index, axis=2)
    first_rows = tiles[:, :, :1, :]
    zero_row = jnp.zeros_like(first_rows[:, :1])
    prev_halo = jnp.concatenate([zero_row, last_rows[:, :-1]], axis=1)
    next_halo = jnp.concatenate([first_rows[:, 1:], zero_row], axis=1)
    prev = jnp.concatenate([prev_halo, tiles[:, :, :-1]], axis=2)
    upper = jnp.concatenate([tiles[:, :, 1:], jnp.zeros_like(first_rows)], axis=2)
    at_end = jnp.arange(TILE_ROWS, dtype=jnp.int32)[None, :] == last_index[:, None]
    after = jnp.where(at_end[None, :, :, None], next_halo, upper)
    return (prev.reshape(field.shape), after.reshape(field.shape))

def tendency(temp, cond, prev_t, prev_k, next_t, next_k, porosity, surf, basal, thickness, live):
    flow = 0.5 * (cond + prev_k) * (prev_t - temp) + 0.5 * (cond + next_k) * (next_t - temp)
    west_t = jnp.concatenate([temp[..., :1], temp[..., :-1]], axis=-1)
    west_k = jnp.concatenate([cond[..., :1], cond[..., :-1]], axis=-1)
    east_t = jnp.concatenate([temp[..., 1:], temp[..., -1:]], axis=-1)
    east_k = jnp.concatenate([cond[..., 1:], cond[..., -1:]], axis=-1)
    flow = flow + 0.5 * (cond + west_k) * (west_t - temp) + 0.5 * (cond + east_k) * (east_t - temp)
    inverse = 1.0 / (thickness * thickness)
    upper_t = jnp.concatenate([temp[:1], temp[:-1]], axis=0)
    upper_k = jnp.concatenate([cond[:1], cond[:-1]], axis=0)
    lower_t = jnp.concatenate([temp[1:], temp[-1:]], axis=0)
    lower_k = jnp.concatenate([cond[1:], cond[-1:]], axis=0)
    vertical = 0.5 * (cond + upper_k) * (upper_t - temp) + 0.5 * (cond + lower_k) * (lower_t - temp)
    flow = flow + vertical * inverse[None]
    layer = jnp.arange(temp.shape[0], dtype=jnp.int32)[:, None, None]
    flow = flow + jnp.where(layer == 0, 2.0 * cond * inverse[None] * (surf[None] - temp), 0.0)
    flow = flow + jnp.where(layer == temp.shape[0] - 1, (basal / thickness)[None], 0.0)
    sig = jax.nn.sigmoid(temp / WIDTH_T)
    capacity = 1.0 + LATENT * porosity * sig * (1.0 - sig)
    return jnp.where(live, temp + STEP * flow / capacity, 0.0)

def reference(start_temp, cotangent, conductivity, porosity, surface_temp, surface_offset, basal_flux, thickness, tile_len):
    live_rows = jnp.arange(TILE_ROWS, dtype=jnp.int32)[None, :] < tile_len[:, None]
    live = live_rows.reshape(-1)[None, :, None]

    def single(temp, cond, offset, surf_base):
        prev_t, next_t = along_ridge(temp, tile_len)
        prev_k, next_k = along_ridge(cond, tile_len)
        return tendency(temp, cond, prev_t, prev_k, next_t, next_k, porosity, surf_base + offset, basal_flux, thickness, live)

    def member(carry, items):
        temp, cot, surf_base = items
        result, pull = jax.vjp(lambda t, c, o: single(t, c, o, surf_base), temp, conductivity, surface_offset)
        grad_t, grad_k, grad_o = pull(cot)
        return ((carry[0] + grad_k, carry[1] + grad_o), (result, grad_t))
    start = (jnp.zeros_like(conductivity), jnp.zeros_like(surface_offset))
    (grad_cond, grad_offset), (heated, adj_temp) = lax.scan(member, start, (start_temp, cotangent, surface_temp))
    new_cond = conductivity * jnp.exp(-RATE * jnp.tanh(grad_cond))
    return (heated, adj_temp, new_cond, grad_offset)
```

```python
import jax
import jax.numpy as jnp
from jax import lax
from jax.experimental import pallas as pl
from jax.experimental.pallas import tpu as pltpu
from jax.sharding import PartitionSpec as P

STEP = 0.03
RATE = 0.5
MESH = pl.DeviceIdType.MESH
CORES = 2


def kernel(
    n_space,
    groups,
    len_ref,
    temp_hbm,
    por_hbm,
    cot_hbm,
    cond_hbm,
    surf_hbm,
    offset_hbm,
    basal_hbm,
    thick_hbm,
    heated_hbm,
    adj_hbm,
    new_hbm,
    goff_hbm,
    temp,
    por,
    cot,
    cond,
    surf,
    offset,
    basal,
    thick,
    inverse,
    weight,
    recip,
    slope,
    heated,
    adj,
    grad,
    near,
    far,
    new,
    edge_out,
    edge_in,
    edge,
    extra_out,
    extra_near,
    extra_far,
    goff,
    in_sem,
    halo_send,
    halo_recv,
    near_send,
    near_recv,
    far_send,
    far_recv,
    new_send,
    new_recv,
    new_local,
    out_sem,
):
    layers, rows, across = temp.shape
    chunks = layers // CORES
    half = rows // CORES
    space = lax.axis_index("space")
    member = lax.axis_index("member")
    core = lax.rem(member, CORES)
    group = lax.div(member, CORES)
    partner = (space, member + 1 - 2 * core)
    peers = [lax.rem(group + d, groups) for d in range(1, groups)]
    peer_ids = [(space, p * CORES + core) for p in peers]
    behind = (space - 1, member)
    ahead = (space + 1, member)
    has_behind = space > 0
    has_ahead = space < n_space - 1

    barrier = pltpu.get_barrier_semaphore()
    for other in [partner] + peer_ids:
        pl.semaphore_signal(barrier, inc=1, device_id=other, device_id_type=MESH)

    @pl.when(has_behind)
    def _():
        pl.semaphore_signal(barrier, inc=1, device_id=behind, device_id_type=MESH)

    @pl.when(has_ahead)
    def _():
        pl.semaphore_signal(barrier, inc=1, device_id=ahead, device_id_type=MESH)

    loads = [
        pltpu.make_async_copy(src, dst, in_sem.at[i])
        for i, (src, dst) in enumerate(
            [
                (temp_hbm, temp),
                (por_hbm, por),
                (cot_hbm, cot),
                (cond_hbm, cond),
                (surf_hbm, surf),
                (offset_hbm, offset),
                (basal_hbm, basal),
                (thick_hbm, thick),
            ]
        )
    ]
    for load in loads:
        load.start()

    count = len_ref[0]
    end = jnp.clip(count - 1, 0, rows - 1)
    row = lax.broadcasted_iota(jnp.int32, (rows, across), 0)
    col = lax.broadcasted_iota(jnp.int32, (rows, across), 1)
    live = row < count
    inner = (row >= 1) & live
    not_east = col < across - 1

    @pl.when(jnp.logical_not(has_behind))
    def _():
        edge_in[0] = jnp.zeros(edge_in.shape[1:], jnp.float32)

    @pl.when(jnp.logical_not(has_ahead))
    def _():
        edge_in[1] = jnp.zeros(edge_in.shape[1:], jnp.float32)

    for load in loads:
        load.wait()

    def pointwise(v, p, c):
        th = jnp.tanh(v)
        q = p * (1.0 - th * th)
        r = 1.0 / (1.0 + 4.0 * q)
        return r, STEP * c * r, 8.0 * th * q

    for layer in range(layers):
        at = pl.ds(layer, 1)
        for f, field in enumerate((temp, cond, cot, por)):
            edge_out[0, f, at, :] = field[layer, 0:1, :]
            edge_out[1, f, at, :] = field[layer, pl.ds(end, 1), :]
    for side in range(2):
        _, w, _ = pointwise(edge_out[side, 0], edge_out[side, 3], edge_out[side, 2])
        edge_out[side, 2] = w

    neighbours = has_behind.astype(jnp.int32) + has_ahead.astype(jnp.int32)
    pl.semaphore_wait(barrier, groups + neighbours)

    to_behind = pltpu.make_async_remote_copy(
        src_ref=edge_out.at[0, 0:3],
        dst_ref=edge_in.at[1],
        send_sem=halo_send.at[0],
        recv_sem=halo_recv.at[1],
        device_id=behind,
        device_id_type=MESH,
    )
    to_ahead = pltpu.make_async_remote_copy(
        src_ref=edge_out.at[1, 0:3],
        dst_ref=edge_in.at[0],
        send_sem=halo_send.at[1],
        recv_sem=halo_recv.at[0],
        device_id=ahead,
        device_id_type=MESH,
    )

    @pl.when(has_behind)
    def _():
        to_behind.start()

    @pl.when(has_ahead)
    def _():
        to_ahead.start()

    inverse[...] = 1.0 / (thick[...] * thick[...])

    def weigh(layer):
        r, w, s = pointwise(temp[layer], por[layer], cot[layer])
        w = jnp.where(live, w, 0.0)
        recip[layer] = r
        weight[layer] = w
        slope[layer] = w * r * s

    def stencil(layer, above, below, top=False, bottom=False):
        v, k, w = temp[layer], cond[layer], weight[layer]

        def east(x):
            return pltpu.roll(x, across - 1, 1)

        def west(x):
            return pltpu.roll(x, 1, 1)

        def prev(x):
            return pltpu.roll(x, 1, 0)

        def following(x):
            return pltpu.roll(x, rows - 1, 0)

        a = jnp.where(not_east, 0.5 * (k + east(k)), 0.0)
        dv = jnp.where(not_east, east(v) - v, 0.0)
        dw = east(w) - w
        f, b, g = a * dv, a * dw, dv * dw
        flow = f - west(f)
        back = b - west(b)
        cross = g + west(g)

        a = jnp.where(inner, 0.5 * (k + prev(k)), 0.0)
        dv = jnp.where(inner, prev(v) - v, 0.0)
        dw = prev(w) - w
        f, b, g = a * dv, a * dw, dv * dw
        flow = flow + (f - following(f))
        back = back + (b - following(b))
        cross = cross + (g + following(g))

        parts = []
        for other in (above, below):
            if other is not None:
                a = 0.5 * (k + cond[other])
                dv = temp[other] - v
                dw = weight[other] - w
                parts.append((a * dv, a * dw, dv * dw))
        f, b, g = parts[0]
        for more in parts[1:]:
            f, b, g = f + more[0], b + more[1], g + more[2]
        inv = inverse[...]
        if top:
            a = 2.0 * k
            dv = surf[...] + offset[...] - v
            f = f + a * dv
            b = b - a * w
            g = g - 4.0 * (dv * w)
            goff[...] = a * inv * w
        flow = flow + f * inv
        back = back + b * inv
        cross = cross + g * inv
        if bottom:
            flow = flow + basal[...] / thick[...]
        heated[layer] = flow
        adj[layer] = back
        grad[layer] = -0.5 * cross

    def near_copy(j):
        return pltpu.make_async_remote_copy(
            src_ref=grad.at[CORES * j + 1 - core],
            dst_ref=near.at[j],
            send_sem=near_send.at[j],
            recv_sem=near_recv.at[j],
            device_id=partner,
            device_id_type=MESH,
        )

    def far_copies(j):
        return [
            pltpu.make_async_remote_copy(
                src_ref=far.at[group, j],
                dst_ref=far.at[group, j],
                send_sem=far_send.at[d, j],
                recv_sem=far_recv.at[group, j],
                device_id=peer_ids[d],
                device_id_type=MESH,
            )
            for d in range(groups - 1)
        ]

    def far_arrivals(j):
        return [
            pltpu.make_async_remote_copy(
                src_ref=far.at[peers[d], j],
                dst_ref=far.at[peers[d], j],
                send_sem=far_send.at[d, j],
                recv_sem=far_recv.at[peers[d], j],
                device_id=peer_ids[d],
                device_id_type=MESH,
            )
            for d in range(groups - 1)
        ]

    def chunk(j, first=False, last=False):
        layer = CORES * j
        if not last:
            weigh(layer + 2)
            weigh(layer + 3)
        stencil(layer, None if first else layer - 1, layer + 1, top=first)
        stencil(layer + 1, layer, None if last else layer + 2, bottom=last)
        near_copy(j).start()

    def pass_on(j):
        near_copy(j).wait_recv()
        far[group, j] = grad[CORES * j + core] + near[j]
        for copy in far_copies(j):
            copy.start()

    def step(j, carry):
        chunk(j)
        pass_on(j - 1)
        return carry

    extra_near_copy = pltpu.make_async_remote_copy(
        src_ref=extra_out.at[1 - core],
        dst_ref=extra_near,
        send_sem=near_send.at[chunks],
        recv_sem=near_recv.at[chunks],
        device_id=partner,
        device_id_type=MESH,
    )

    def extra_far_copy(d, slot):
        return pltpu.make_async_remote_copy(
            src_ref=extra_far.at[slot],
            dst_ref=extra_far.at[slot],
            send_sem=far_send.at[d, chunks],
            recv_sem=far_recv.at[slot, chunks],
            device_id=peer_ids[d],
            device_id_type=MESH,
        )

    weigh(0)
    weigh(1)
    chunk(0, first=True)
    middle = chunks // 2
    lax.fori_loop(1, middle, step, 0)

    @pl.when(has_ahead)
    def _():
        to_behind.wait_recv()

    @pl.when(has_behind)
    def _():
        to_ahead.wait_recv()

    for side in range(2):
        a = 0.5 * (edge_out[side, 1] + edge_in[side, 1])
        dv = edge_in[side, 0] - edge_out[side, 0]
        dw = edge_in[side, 2] - edge_out[side, 2]
        edge[side, 0] = a * dv
        edge[side, 1] = a * dw
        g = -0.5 * (dv * dw)
        for layer in range(layers):
            at = side * chunks + layer // CORES
            extra_out[layer % CORES, at : at + 1, :] = g[layer : layer + 1, :]
    for h in range(CORES):
        extra_out[h, layers : layers + half, :] = goff[h * half : (h + 1) * half, :]
    extra_near_copy.start()

    lax.fori_loop(middle, chunks - 1, step, 0)
    extra_near_copy.wait_recv()
    extra_far[group] = extra_out[core] + extra_near[...]
    for d in range(groups - 1):
        extra_far_copy(d, group).start()
    chunk(chunks - 1, last=True)
    pass_on(chunks - 2)

    first_row = row == 0
    last_row = row == count - 1

    def out_copies(layer):
        return (
            pltpu.make_async_copy(heated.at[layer], heated_hbm.at[layer], out_sem.at[0, layer]),
            pltpu.make_async_copy(adj.at[layer], adj_hbm.at[layer], out_sem.at[1, layer]),
        )

    def finish(layer, carry):
        at = pl.ds(layer, 1)

        def edges(f):
            return jnp.where(first_row, edge[0, f, at, :], 0.0) + jnp.where(
                last_row, edge[1, f, at, :], 0.0
            )

        flow = heated[layer] + edges(0)
        heated[layer] = jnp.where(live, temp[layer] + STEP * (flow * recip[layer]), 0.0)
        adj[layer] = jnp.where(
            live, cot[layer] + (adj[layer] + edges(1) + slope[layer] * flow), 0.0
        )
        for copy in out_copies(layer):
            copy.start()
        return carry

    lax.fori_loop(0, 4, finish, 0)
    pass_on(chunks - 1)
    lax.fori_loop(4, layers, finish, 0)

    for d in range(groups - 1):
        extra_far_copy(d, peers[d]).wait_recv()
    total = extra_far[0]
    for p in range(1, groups):
        total = total + extra_far[p]
    extra_near[...] = total
    mine = pl.ds(pl.multiple_of(core * half, half), half)
    goff_local = pltpu.make_async_copy(
        extra_near.at[pl.ds(layers, half)], goff_hbm.at[mine], new_local.at[chunks]
    )
    goff_remote = pltpu.make_async_remote_copy(
        src_ref=extra_near.at[pl.ds(layers, half)],
        dst_ref=goff_hbm.at[mine],
        send_sem=new_send.at[chunks],
        recv_sem=new_recv.at[chunks],
        device_id=partner,
        device_id_type=MESH,
    )
    goff_local.start()
    goff_remote.start()

    def new_copies(j):
        layer = CORES * j + core
        return (
            pltpu.make_async_copy(new.at[j], new_hbm.at[layer], new_local.at[j]),
            pltpu.make_async_remote_copy(
                src_ref=new.at[j],
                dst_ref=new_hbm.at[layer],
                send_sem=new_send.at[j],
                recv_sem=new_recv.at[j],
                device_id=partner,
                device_id_type=MESH,
            ),
        )

    def update(j, carry):
        for copy in far_arrivals(j):
            copy.wait_recv()
        total = far[0, j]
        for p in range(1, groups):
            total = total + far[p, j]
        total = total + jnp.where(first_row, extra_near[pl.ds(j, 1), :], 0.0)
        total = total + jnp.where(last_row, extra_near[pl.ds(chunks + j, 1), :], 0.0)
        new[j] = cond[CORES * j + core] * jnp.exp(-RATE * jnp.tanh(total))
        for copy in new_copies(j):
            copy.start()
        return carry

    lax.fori_loop(0, chunks, update, 0)

    def drain(j, carry):
        near_copy(j).wait_send()
        for copy in far_copies(j):
            copy.wait_send()
        local, remote = new_copies(j)
        local.wait()
        remote.wait()
        return carry

    def drain_out(layer, carry):
        for copy in out_copies(layer):
            copy.wait()
        return carry

    @pl.when(has_behind)
    def _():
        to_behind.wait_send()

    @pl.when(has_ahead)
    def _():
        to_ahead.wait_send()

    extra_near_copy.wait_send()
    for d in range(groups - 1):
        extra_far_copy(d, group).wait_send()
    lax.fori_loop(0, layers, drain_out, 0)
    lax.fori_loop(0, chunks, drain, 0)
    goff_local.wait()
    goff_remote.wait()


def solution(mesh):
    n_space, n_member = mesh.shape["space"], mesh.shape["member"]
    groups = n_member // CORES

    def body(
        start_temp,
        cotangent,
        conductivity,
        porosity,
        surface_temp,
        surface_offset,
        basal_flux,
        thickness,
        tile_len,
    ):
        layers, rows, across = conductivity.shape
        chunks = layers // CORES
        half = rows // CORES
        extra = layers + half
        f32 = jnp.float32
        whole = (layers, rows, across)
        plane = (rows, across)
        dma = pltpu.SemaphoreType.DMA

        def vmem(*shape):
            return pltpu.VMEM(shape, f32)

        hbm = pl.BlockSpec(memory_space=pltpu.HBM)
        either = pl.BlockSpec(memory_space=pl.ANY)
        cells = layers * rows * across
        heated, adj, new, goff = pl.pallas_call(
            lambda *refs: kernel(n_space, groups, *refs),
            out_shape=[jax.ShapeDtypeStruct(s, f32) for s in (whole, whole, whole, plane)],
            in_specs=[pl.BlockSpec(memory_space=pltpu.SMEM)] + [hbm] * 8,
            out_specs=[either] * 4,
            scratch_shapes=[vmem(*whole)] * 4
            + [vmem(*plane)] * 5
            + [vmem(*whole)] * 6
            + [
                vmem(chunks, *plane),
                vmem(groups, chunks, *plane),
                vmem(chunks, *plane),
                vmem(2, 4, layers, across),
                vmem(2, 3, layers, across),
                vmem(2, 2, layers, across),
                vmem(CORES, extra, across),
                vmem(extra, across),
                vmem(groups, extra, across),
                vmem(*plane),
                dma((8,)),
                dma((2,)),
                dma((2,)),
                dma((chunks + 1,)),
                dma((chunks + 1,)),
                dma((max(groups - 1, 1), chunks + 1)),
                dma((groups, chunks + 1)),
                dma((chunks + 1,)),
                dma((chunks + 1,)),
                dma((chunks + 1,)),
                dma((2, layers)),
            ],
            compiler_params=pltpu.CompilerParams(
                collective_id=0, has_side_effects=True, vmem_limit_bytes=62 * 1024 * 1024
            ),
            cost_estimate=pl.CostEstimate(
                flops=100 * cells, bytes_accessed=28 * cells, transcendentals=3 * cells
            ),
            name="heat_step",
        )(
            tile_len,
            start_temp[0],
            porosity,
            cotangent[0],
            conductivity,
            surface_temp[0],
            surface_offset,
            basal_flux,
            thickness,
        )
        return heated[None], adj[None], new, goff

    in_specs = (
        P("member", None, "space", None),
        P("member", None, "space", None),
        P(None, "space", None),
        P(None, "space", None),
        P("member", "space", None),
        P("space", None),
        P("space", None),
        P("space", None),
        P("space"),
    )
    out_specs = (
        P("member", None, "space", None),
        P("member", None, "space", None),
        P(None, "space", None),
        P("space", None),
    )
    return jax.shard_map(body, mesh=mesh, in_specs=in_specs, out_specs=out_specs, check_vma=False)
```

```python
import jax
import jax.numpy as jnp
from jax import lax
from jax.experimental import pallas as pl
from jax.experimental.pallas import tpu as pltpu
from jax.sharding import PartitionSpec as P

STEP = 0.03
RATE = 0.5
MESH = pl.DeviceIdType.MESH
CORES = 2


def kernel(
    n_space,
    groups,
    len_ref,
    temp_hbm,
    por_hbm,
    cot_hbm,
    cond_hbm,
    surf_hbm,
    offset_hbm,
    basal_hbm,
    thick_hbm,
    heated,
    adj,
    new,
    goff,
    temp,
    por,
    cot,
    cond,
    surf,
    offset,
    basal,
    thick,
    inverse,
    weight,
    recip,
    slope,
    grad,
    near,
    far,
    edge_out,
    edge_in,
    edge,
    extra_out,
    extra_near,
    extra_far,
    goff_mine,
    in_sem,
    halo_send,
    halo_recv,
    near_send,
    near_recv,
    far_send,
    far_recv,
    new_send,
    new_recv,
):
    layers, rows, across = temp.shape
    chunks = layers // CORES
    half = rows // CORES
    space = lax.axis_index("space")
    member = lax.axis_index("member")
    core = lax.rem(member, CORES)
    group = lax.div(member, CORES)
    partner = (space, member + 1 - 2 * core)
    peers = [lax.rem(group + d, groups) for d in range(1, groups)]
    peer_ids = [(space, p * CORES + core) for p in peers]
    behind = (space - 1, member)
    ahead = (space + 1, member)
    has_behind = space > 0
    has_ahead = space < n_space - 1

    barrier = pltpu.get_barrier_semaphore()
    for other in [partner] + peer_ids:
        pl.semaphore_signal(barrier, inc=1, device_id=other, device_id_type=MESH)

    @pl.when(has_behind)
    def _():
        pl.semaphore_signal(barrier, inc=1, device_id=behind, device_id_type=MESH)

    @pl.when(has_ahead)
    def _():
        pl.semaphore_signal(barrier, inc=1, device_id=ahead, device_id_type=MESH)

    early = 2 * CORES
    fields = [(temp_hbm, temp), (por_hbm, por), (cot_hbm, cot), (cond_hbm, cond)]
    planes = [(thick_hbm, thick), (surf_hbm, surf), (offset_hbm, offset), (basal_hbm, basal)]
    pieces = [(src.at[0:early], dst.at[0:early]) for src, dst in fields]
    pieces += planes
    n_first = len(pieces)
    pieces += [(src.at[early:layers], dst.at[early:layers]) for src, dst in fields]
    loads = [
        pltpu.make_async_copy(src, dst, in_sem.at[i]) for i, (src, dst) in enumerate(pieces)
    ]
    for load in loads:
        load.start()

    @pl.when(jnp.logical_not(has_behind))
    def _():
        edge_in[0] = jnp.zeros(edge_in.shape[1:], jnp.float32)

    @pl.when(jnp.logical_not(has_ahead))
    def _():
        edge_in[1] = jnp.zeros(edge_in.shape[1:], jnp.float32)

    for load in loads[:n_first]:
        load.wait()
    count = len_ref[0]
    end = jnp.clip(count - 1, 0, rows - 1)
    row = lax.broadcasted_iota(jnp.int32, (rows, across), 0)
    col = lax.broadcasted_iota(jnp.int32, (rows, across), 1)
    live = row < count
    inner = (row >= 1) & live
    not_east = col < across - 1
    inverse[...] = 1.0 / (thick[...] * thick[...])

    def pointwise(v, p, c):
        th = jnp.tanh(v)
        q = p * (1.0 - th * th)
        r = 1.0 / (1.0 + 4.0 * q)
        return r, STEP * c * r, 8.0 * th * q

    to_behind = pltpu.make_async_remote_copy(
        src_ref=edge_out.at[0, 0:3],
        dst_ref=edge_in.at[1],
        send_sem=halo_send.at[0],
        recv_sem=halo_recv.at[1],
        device_id=behind,
        device_id_type=MESH,
    )
    to_ahead = pltpu.make_async_remote_copy(
        src_ref=edge_out.at[1, 0:3],
        dst_ref=edge_in.at[0],
        send_sem=halo_send.at[1],
        recv_sem=halo_recv.at[0],
        device_id=ahead,
        device_id_type=MESH,
    )

    def weigh(layer):
        r, w, s = pointwise(temp[layer], por[layer], cot[layer])
        w = jnp.where(live, w, 0.0)
        recip[layer] = r
        weight[layer] = w
        slope[layer] = w * r * s

    def stencil(layer, above, below, top=False, bottom=False):
        v, k, w = temp[layer], cond[layer], weight[layer]

        def east(x):
            return pltpu.roll(x, across - 1, 1)

        def west(x):
            return pltpu.roll(x, 1, 1)

        def prev(x):
            return pltpu.roll(x, 1, 0)

        def following(x):
            return pltpu.roll(x, rows - 1, 0)

        a = jnp.where(not_east, 0.5 * (k + east(k)), 0.0)
        dv = jnp.where(not_east, east(v) - v, 0.0)
        dw = east(w) - w
        f, b, g = a * dv, a * dw, dv * dw
        flow = f - west(f)
        back = b - west(b)
        cross = g + west(g)

        a = jnp.where(inner, 0.5 * (k + prev(k)), 0.0)
        dv = jnp.where(inner, prev(v) - v, 0.0)
        dw = prev(w) - w
        f, b, g = a * dv, a * dw, dv * dw
        flow = flow + (f - following(f))
        back = back + (b - following(b))
        cross = cross + (g + following(g))

        parts = []
        for other in (above, below):
            if other is not None:
                a = 0.5 * (k + cond[other])
                dv = temp[other] - v
                dw = weight[other] - w
                parts.append((a * dv, a * dw, dv * dw))
        f, b, g = parts[0]
        for more in parts[1:]:
            f, b, g = f + more[0], b + more[1], g + more[2]
        inv = inverse[...]
        if top:
            a = 2.0 * k
            dv = surf[...] + offset[...] - v
            f = f + a * dv
            b = b - a * w
            g = g - 4.0 * (dv * w)
            goff_mine[...] = a * inv * w
        flow = flow + f * inv
        back = back + b * inv
        cross = cross + g * inv
        if bottom:
            flow = flow + basal[...] / thick[...]
        heated[layer] = flow
        adj[layer] = back
        grad[layer] = -0.5 * cross

    neighbours = has_behind.astype(jnp.int32) + has_ahead.astype(jnp.int32)

    def near_copy(j):
        return pltpu.make_async_remote_copy(
            src_ref=grad.at[CORES * j + 1 - core],
            dst_ref=near.at[j],
            send_sem=near_send.at[j],
            recv_sem=near_recv.at[j],
            device_id=partner,
            device_id_type=MESH,
        )

    def far_copies(j):
        return [
            pltpu.make_async_remote_copy(
                src_ref=far.at[group, j],
                dst_ref=far.at[group, j],
                send_sem=far_send.at[d, j],
                recv_sem=far_recv.at[group, j],
                device_id=peer_ids[d],
                device_id_type=MESH,
            )
            for d in range(groups - 1)
        ]

    def far_arrivals(j):
        return [
            pltpu.make_async_remote_copy(
                src_ref=far.at[peers[d], j],
                dst_ref=far.at[peers[d], j],
                send_sem=far_send.at[d, j],
                recv_sem=far_recv.at[peers[d], j],
                device_id=peer_ids[d],
                device_id_type=MESH,
            )
            for d in range(groups - 1)
        ]

    def chunk(j, first=False, last=False):
        layer = CORES * j
        if not last:
            weigh(layer + 2)
            weigh(layer + 3)
        stencil(layer, None if first else layer - 1, layer + 1, top=first)
        stencil(layer + 1, layer, None if last else layer + 2, bottom=last)
        if first:
            pl.semaphore_wait(barrier, groups + neighbours)
        near_copy(j).start()

    def pass_on(j):
        near_copy(j).wait_recv()
        far[group, j] = grad[CORES * j + core] + near[j]
        for copy in far_copies(j):
            copy.start()

    def step(j, carry):
        chunk(j)
        pass_on(j - 1)
        return carry

    extra_near_copy = pltpu.make_async_remote_copy(
        src_ref=extra_out.at[1 - core],
        dst_ref=extra_near,
        send_sem=near_send.at[chunks],
        recv_sem=near_recv.at[chunks],
        device_id=partner,
        device_id_type=MESH,
    )

    def extra_far_copy(d, slot):
        return pltpu.make_async_remote_copy(
            src_ref=extra_far.at[slot],
            dst_ref=extra_far.at[slot],
            send_sem=far_send.at[d, chunks],
            recv_sem=far_recv.at[slot, chunks],
            device_id=peer_ids[d],
            device_id_type=MESH,
        )

    weigh(0)
    weigh(1)
    chunk(0, first=True)
    for load in loads[n_first:]:
        load.wait()

    for layer in range(layers):
        at = pl.ds(layer, 1)
        for f, field in enumerate((temp, cond, cot, por)):
            edge_out[0, f, at, :] = field[layer, 0:1, :]
            edge_out[1, f, at, :] = field[layer, pl.ds(end, 1), :]
    for side in range(2):
        _, w, _ = pointwise(edge_out[side, 0], edge_out[side, 3], edge_out[side, 2])
        edge_out[side, 2] = w

    @pl.when(has_behind)
    def _():
        to_behind.start()

    @pl.when(has_ahead)
    def _():
        to_ahead.start()

    middle = chunks // 2
    lax.fori_loop(1, middle, step, 0)

    @pl.when(has_ahead)
    def _():
        to_behind.wait_recv()

    @pl.when(has_behind)
    def _():
        to_ahead.wait_recv()

    for side in range(2):
        a = 0.5 * (edge_out[side, 1] + edge_in[side, 1])
        dv = edge_in[side, 0] - edge_out[side, 0]
        dw = edge_in[side, 2] - edge_out[side, 2]
        edge[side, 0] = a * dv
        edge[side, 1] = a * dw
        g = -0.5 * (dv * dw)
        for layer in range(layers):
            at = side * chunks + layer // CORES
            extra_out[layer % CORES, at : at + 1, :] = g[layer : layer + 1, :]
    for h in range(CORES):
        extra_out[h, layers : layers + half, :] = goff_mine[h * half : (h + 1) * half, :]
    extra_near_copy.start()

    lax.fori_loop(middle, chunks - 1, step, 0)
    extra_near_copy.wait_recv()
    extra_far[group] = extra_out[core] + extra_near[...]
    for d in range(groups - 1):
        extra_far_copy(d, group).start()
    chunk(chunks - 1, last=True)
    pass_on(chunks - 2)

    first_row = row == 0
    last_row = row == count - 1

    def finish(layer, carry):
        at = pl.ds(layer, 1)

        def edges(f):
            return jnp.where(first_row, edge[0, f, at, :], 0.0) + jnp.where(
                last_row, edge[1, f, at, :], 0.0
            )

        flow = heated[layer] + edges(0)
        heated[layer] = jnp.where(live, temp[layer] + STEP * (flow * recip[layer]), 0.0)
        adj[layer] = jnp.where(
            live, cot[layer] + (adj[layer] + edges(1) + slope[layer] * flow), 0.0
        )
        return carry

    lax.fori_loop(0, 4, finish, 0)
    pass_on(chunks - 1)
    lax.fori_loop(4, layers, finish, 0)

    for d in range(groups - 1):
        extra_far_copy(d, peers[d]).wait_recv()
    total = extra_far[0]
    for p in range(1, groups):
        total = total + extra_far[p]
    extra_near[...] = total
    mine = pl.ds(pl.multiple_of(core * half, half), half)
    other = pl.ds(pl.multiple_of((1 - core) * half, half), half)
    goff[mine, :] = total[layers : layers + half]
    goff_remote = pltpu.make_async_remote_copy(
        src_ref=goff.at[mine],
        dst_ref=goff.at[mine],
        send_sem=new_send.at[chunks],
        recv_sem=new_recv.at[chunks],
        device_id=partner,
        device_id_type=MESH,
    )
    goff_remote.start()

    def new_copy(j):
        layer = CORES * j + core
        return pltpu.make_async_remote_copy(
            src_ref=new.at[layer],
            dst_ref=new.at[layer],
            send_sem=new_send.at[j],
            recv_sem=new_recv.at[j],
            device_id=partner,
            device_id_type=MESH,
        )

    def new_arrival(j):
        layer = CORES * j + 1 - core
        return pltpu.make_async_remote_copy(
            src_ref=new.at[layer],
            dst_ref=new.at[layer],
            send_sem=new_send.at[j],
            recv_sem=new_recv.at[j],
            device_id=partner,
            device_id_type=MESH,
        )

    def update(j, carry):
        for copy in far_arrivals(j):
            copy.wait_recv()
        total = far[0, j]
        for p in range(1, groups):
            total = total + far[p, j]
        total = total + jnp.where(first_row, extra_near[pl.ds(j, 1), :], 0.0)
        total = total + jnp.where(last_row, extra_near[pl.ds(chunks + j, 1), :], 0.0)
        layer = CORES * j + core
        new[layer] = cond[layer] * jnp.exp(-RATE * jnp.tanh(total))
        new_copy(j).start()
        return carry

    lax.fori_loop(0, chunks, update, 0)

    def drain(j, carry):
        near_copy(j).wait_send()
        for copy in far_copies(j):
            copy.wait_send()
        new_copy(j).wait_send()
        new_arrival(j).wait_recv()
        return carry

    @pl.when(has_behind)
    def _():
        to_behind.wait_send()

    @pl.when(has_ahead)
    def _():
        to_ahead.wait_send()

    extra_near_copy.wait_send()
    for d in range(groups - 1):
        extra_far_copy(d, group).wait_send()
    lax.fori_loop(0, chunks, drain, 0)
    goff_remote.wait_send()
    pltpu.make_async_remote_copy(
        src_ref=goff.at[other],
        dst_ref=goff.at[other],
        send_sem=new_send.at[chunks],
        recv_sem=new_recv.at[chunks],
        device_id=partner,
        device_id_type=MESH,
    ).wait_recv()


def write_out(*refs):
    sources, targets, sem = refs[:4], refs[4:8], refs[8]
    copies = [
        pltpu.make_async_copy(src, dst, sem.at[i])
        for i, (src, dst) in enumerate(zip(sources, targets))
    ]
    for copy in copies:
        copy.start()
    for copy in copies:
        copy.wait()


def solution(mesh):
    n_space, n_member = mesh.shape["space"], mesh.shape["member"]
    groups = n_member // CORES

    def body(
        start_temp,
        cotangent,
        conductivity,
        porosity,
        surface_temp,
        surface_offset,
        basal_flux,
        thickness,
        tile_len,
    ):
        layers, rows, across = conductivity.shape
        chunks = layers // CORES
        half = rows // CORES
        extra = layers + half
        f32 = jnp.float32
        whole = (layers, rows, across)
        plane = (rows, across)
        dma = pltpu.SemaphoreType.DMA

        def vmem(*shape):
            return pltpu.VMEM(shape, f32)

        hbm = pl.BlockSpec(memory_space=pltpu.HBM)
        either = pl.BlockSpec(memory_space=pl.ANY)
        cells = layers * rows * across
        heated, adj, new, goff = pl.pallas_call(
            lambda *refs: kernel(n_space, groups, *refs),
            out_shape=[pltpu.VMEM(s, f32) for s in (whole, whole, whole, plane)],
            in_specs=[pl.BlockSpec(memory_space=pltpu.SMEM)] + [hbm] * 8,
            out_specs=[pl.BlockSpec(memory_space=pltpu.VMEM)] * 4,
            scratch_shapes=[vmem(*whole)] * 4
            + [vmem(*plane)] * 5
            + [vmem(*whole)] * 4
            + [
                vmem(chunks, *plane),
                vmem(groups, chunks, *plane),
                vmem(2, 4, layers, across),
                vmem(2, 3, layers, across),
                vmem(2, 2, layers, across),
                vmem(CORES, extra, across),
                vmem(extra, across),
                vmem(groups, extra, across),
                vmem(*plane),
                dma((12,)),
                dma((2,)),
                dma((2,)),
                dma((chunks + 1,)),
                dma((chunks + 1,)),
                dma((max(groups - 1, 1), chunks + 1)),
                dma((groups, chunks + 1)),
                dma((chunks + 1,)),
                dma((chunks + 1,)),
            ],
            compiler_params=pltpu.CompilerParams(
                collective_id=0, has_side_effects=True, vmem_limit_bytes=48 * 1024 * 1024
            ),
            cost_estimate=pl.CostEstimate(
                flops=100 * cells, bytes_accessed=28 * cells, transcendentals=3 * cells
            ),
            name="heat_step",
        )(
            tile_len,
            *[
                pltpu.with_memory_space_constraint(x, pltpu.HBM)
                for x in (
                    start_temp[0],
                    porosity,
                    cotangent[0],
                    conductivity,
                    surface_temp[0],
                    surface_offset,
                    basal_flux,
                    thickness,
                )
            ]
        )
        heated, adj, new, goff = pl.pallas_call(
            write_out,
            out_shape=[pltpu.HBM(s, f32) for s in (whole, whole, whole, plane)],
            in_specs=[either] * 4,
            out_specs=[hbm] * 4,
            scratch_shapes=[dma((4,))],
            cost_estimate=pl.CostEstimate(flops=0, bytes_accessed=24 * cells, transcendentals=0),
            name="write_out",
        )(heated, adj, new, goff)
        return heated[None], adj[None], new, goff

    in_specs = (
        P("member", None, "space", None),
        P("member", None, "space", None),
        P(None, "space", None),
        P(None, "space", None),
        P("member", "space", None),
        P("space", None),
        P("space", None),
        P("space", None),
        P("space"),
    )
    out_specs = (
        P("member", None, "space", None),
        P("member", None, "space", None),
        P(None, "space", None),
        P("space", None),
    )
    return jax.shard_map(body, mesh=mesh, in_specs=in_specs, out_specs=out_specs, check_vma=False)
```

```python
import jax
import jax.numpy as jnp
from jax import lax
from jax.experimental import pallas as pl
from jax.experimental.pallas import tpu as pltpu
from jax.sharding import PartitionSpec as P

STEP = 0.03
RATE = 0.5
MESH = pl.DeviceIdType.MESH
CORES = 2


def kernel(
    n_space,
    groups,
    len_ref,
    temp_hbm,
    por_hbm,
    cot_hbm,
    cond_hbm,
    surf_hbm,
    offset_hbm,
    basal_hbm,
    thick_hbm,
    heated,
    adj,
    new,
    goff,
    temp,
    por,
    cot,
    cond,
    surf,
    offset,
    basal,
    thick,
    inverse,
    weight,
    recip,
    slope,
    grad,
    near,
    far,
    edge_out,
    edge_in,
    edge,
    extra_out,
    extra_near,
    extra_far,
    goff_mine,
    in_sem,
    halo_send,
    halo_recv,
    near_send,
    near_recv,
    far_send,
    far_recv,
    new_send,
    new_recv,
):
    layers, rows, across = temp.shape
    chunks = layers // CORES
    half = rows // CORES
    space = lax.axis_index("space")
    member = lax.axis_index("member")
    core = lax.rem(member, CORES)
    group = lax.div(member, CORES)
    partner = (space, member + 1 - 2 * core)
    peers = [lax.rem(group + d, groups) for d in range(1, groups)]
    peer_ids = [(space, p * CORES + core) for p in peers]
    behind = (space - 1, member)
    ahead = (space + 1, member)
    has_behind = space > 0
    has_ahead = space < n_space - 1

    barrier = pltpu.get_barrier_semaphore()
    for other in [partner] + peer_ids:
        pl.semaphore_signal(barrier, inc=1, device_id=other, device_id_type=MESH)

    @pl.when(has_behind)
    def _():
        pl.semaphore_signal(barrier, inc=1, device_id=behind, device_id_type=MESH)

    @pl.when(has_ahead)
    def _():
        pl.semaphore_signal(barrier, inc=1, device_id=ahead, device_id_type=MESH)

    cuts = [0, 2 * CORES, 4 * CORES, layers]
    fields = [(temp_hbm, temp), (por_hbm, por), (cot_hbm, cot), (cond_hbm, cond)]
    planes = [(thick_hbm, thick), (surf_hbm, surf), (offset_hbm, offset), (basal_hbm, basal)]
    parts = [
        [(src.at[lo:hi], dst.at[lo:hi]) for src, dst in fields] for lo, hi in zip(cuts, cuts[1:])
    ]
    parts[0] += planes
    loads = [
        [pltpu.make_async_copy(src, dst, in_sem.at[p, i]) for i, (src, dst) in enumerate(part)]
        for p, part in enumerate(parts)
    ]
    for part in loads:
        for load in part:
            load.start()

    @pl.when(jnp.logical_not(has_behind))
    def _():
        edge_in[0] = jnp.zeros(edge_in.shape[1:], jnp.float32)

    @pl.when(jnp.logical_not(has_ahead))
    def _():
        edge_in[1] = jnp.zeros(edge_in.shape[1:], jnp.float32)

    for load in loads[0]:
        load.wait()
    count = len_ref[0]
    end = jnp.clip(count - 1, 0, rows - 1)
    row = lax.broadcasted_iota(jnp.int32, (rows, across), 0)
    col = lax.broadcasted_iota(jnp.int32, (rows, across), 1)
    live = row < count
    inner = (row >= 1) & live
    not_east = col < across - 1
    inverse[...] = 1.0 / (thick[...] * thick[...])

    def pointwise(v, p, c):
        th = jnp.tanh(v)
        q = p * (1.0 - th * th)
        r = 1.0 / (1.0 + 4.0 * q)
        return r, STEP * c * r, 8.0 * th * q

    to_behind = pltpu.make_async_remote_copy(
        src_ref=edge_out.at[0, 0:3],
        dst_ref=edge_in.at[1],
        send_sem=halo_send.at[0],
        recv_sem=halo_recv.at[1],
        device_id=behind,
        device_id_type=MESH,
    )
    to_ahead = pltpu.make_async_remote_copy(
        src_ref=edge_out.at[1, 0:3],
        dst_ref=edge_in.at[0],
        send_sem=halo_send.at[1],
        recv_sem=halo_recv.at[0],
        device_id=ahead,
        device_id_type=MESH,
    )

    def weigh(layer):
        r, w, s = pointwise(temp[layer], por[layer], cot[layer])
        w = jnp.where(live, w, 0.0)
        recip[layer] = r
        weight[layer] = w
        slope[layer] = w * r * s

    def stencil(layer, above, below, top=False, bottom=False):
        v, k, w = temp[layer], cond[layer], weight[layer]

        def east(x):
            return pltpu.roll(x, across - 1, 1)

        def west(x):
            return pltpu.roll(x, 1, 1)

        def prev(x):
            return pltpu.roll(x, 1, 0)

        def following(x):
            return pltpu.roll(x, rows - 1, 0)

        a = jnp.where(not_east, 0.5 * (k + east(k)), 0.0)
        dv = jnp.where(not_east, east(v) - v, 0.0)
        dw = east(w) - w
        f, b, g = a * dv, a * dw, dv * dw
        flow = f - west(f)
        back = b - west(b)
        cross = g + west(g)

        a = jnp.where(inner, 0.5 * (k + prev(k)), 0.0)
        dv = jnp.where(inner, prev(v) - v, 0.0)
        dw = prev(w) - w
        f, b, g = a * dv, a * dw, dv * dw
        flow = flow + (f - following(f))
        back = back + (b - following(b))
        cross = cross + (g + following(g))

        parts = []
        for other in (above, below):
            if other is not None:
                a = 0.5 * (k + cond[other])
                dv = temp[other] - v
                dw = weight[other] - w
                parts.append((a * dv, a * dw, dv * dw))
        f, b, g = parts[0]
        for more in parts[1:]:
            f, b, g = f + more[0], b + more[1], g + more[2]
        inv = inverse[...]
        if top:
            a = 2.0 * k
            dv = surf[...] + offset[...] - v
            f = f + a * dv
            b = b - a * w
            g = g - 4.0 * (dv * w)
            goff_mine[...] = a * inv * w
        flow = flow + f * inv
        back = back + b * inv
        cross = cross + g * inv
        if bottom:
            flow = flow + basal[...] / thick[...]
        heated[layer] = flow
        adj[layer] = back
        grad[layer] = -0.5 * cross

    neighbours = has_behind.astype(jnp.int32) + has_ahead.astype(jnp.int32)

    def near_copy(j):
        return pltpu.make_async_remote_copy(
            src_ref=grad.at[CORES * j + 1 - core],
            dst_ref=near.at[j],
            send_sem=near_send.at[j],
            recv_sem=near_recv.at[j],
            device_id=partner,
            device_id_type=MESH,
        )

    def far_copies(j):
        return [
            pltpu.make_async_remote_copy(
                src_ref=far.at[group, j],
                dst_ref=far.at[group, j],
                send_sem=far_send.at[d, j],
                recv_sem=far_recv.at[group, j],
                device_id=peer_ids[d],
                device_id_type=MESH,
            )
            for d in range(groups - 1)
        ]

    def far_arrivals(j):
        return [
            pltpu.make_async_remote_copy(
                src_ref=far.at[peers[d], j],
                dst_ref=far.at[peers[d], j],
                send_sem=far_send.at[d, j],
                recv_sem=far_recv.at[peers[d], j],
                device_id=peer_ids[d],
                device_id_type=MESH,
            )
            for d in range(groups - 1)
        ]

    def chunk(j, first=False, last=False):
        layer = CORES * j
        if not last:
            weigh(layer + 2)
            weigh(layer + 3)
        stencil(layer, None if first else layer - 1, layer + 1, top=first)
        stencil(layer + 1, layer, None if last else layer + 2, bottom=last)
        if first:
            pl.semaphore_wait(barrier, groups + neighbours)
        near_copy(j).start()

    def pass_on(j):
        near_copy(j).wait_recv()
        far[group, j] = grad[CORES * j + core] + near[j]
        for copy in far_copies(j):
            copy.start()

    def step(j, carry):
        chunk(j)
        pass_on(j - 2)
        return carry

    extra_near_copy = pltpu.make_async_remote_copy(
        src_ref=extra_out.at[1 - core],
        dst_ref=extra_near,
        send_sem=near_send.at[chunks],
        recv_sem=near_recv.at[chunks],
        device_id=partner,
        device_id_type=MESH,
    )

    def extra_far_copy(d, slot):
        return pltpu.make_async_remote_copy(
            src_ref=extra_far.at[slot],
            dst_ref=extra_far.at[slot],
            send_sem=far_send.at[d, chunks],
            recv_sem=far_recv.at[slot, chunks],
            device_id=peer_ids[d],
            device_id_type=MESH,
        )

    weigh(0)
    weigh(1)
    chunk(0, first=True)
    for load in loads[1]:
        load.wait()
    chunk(1)
    for load in loads[2]:
        load.wait()

    for layer in range(layers):
        at = pl.ds(layer, 1)
        for f, field in enumerate((temp, cond, cot, por)):
            edge_out[0, f, at, :] = field[layer, 0:1, :]
            edge_out[1, f, at, :] = field[layer, pl.ds(end, 1), :]
    for side in range(2):
        _, w, _ = pointwise(edge_out[side, 0], edge_out[side, 3], edge_out[side, 2])
        edge_out[side, 2] = w

    @pl.when(has_behind)
    def _():
        to_behind.start()

    @pl.when(has_ahead)
    def _():
        to_ahead.start()

    middle = chunks // 2
    lax.fori_loop(2, middle, step, 0)

    @pl.when(has_ahead)
    def _():
        to_behind.wait_recv()

    @pl.when(has_behind)
    def _():
        to_ahead.wait_recv()

    for side in range(2):
        a = 0.5 * (edge_out[side, 1] + edge_in[side, 1])
        dv = edge_in[side, 0] - edge_out[side, 0]
        dw = edge_in[side, 2] - edge_out[side, 2]
        edge[side, 0] = a * dv
        edge[side, 1] = a * dw
        g = -0.5 * (dv * dw)
        for layer in range(layers):
            at = side * chunks + layer // CORES
            extra_out[layer % CORES, at : at + 1, :] = g[layer : layer + 1, :]
    for h in range(CORES):
        extra_out[h, layers : layers + half, :] = goff_mine[h * half : (h + 1) * half, :]
    extra_near_copy.start()

    lax.fori_loop(middle, chunks - 1, step, 0)
    extra_near_copy.wait_recv()
    extra_far[group] = extra_out[core] + extra_near[...]
    for d in range(groups - 1):
        extra_far_copy(d, group).start()
    chunk(chunks - 1, last=True)
    pass_on(chunks - 3)

    first_row = row == 0
    last_row = row == count - 1

    def finish(layer, carry):
        at = pl.ds(layer, 1)

        def edges(f):
            return jnp.where(first_row, edge[0, f, at, :], 0.0) + jnp.where(
                last_row, edge[1, f, at, :], 0.0
            )

        flow = heated[layer] + edges(0)
        heated[layer] = jnp.where(live, temp[layer] + STEP * (flow * recip[layer]), 0.0)
        adj[layer] = jnp.where(
            live, cot[layer] + (adj[layer] + edges(1) + slope[layer] * flow), 0.0
        )
        return carry

    pass_on(chunks - 2)
    lax.fori_loop(0, 4, finish, 0)
    pass_on(chunks - 1)
    lax.fori_loop(4, layers, finish, 0)

    for d in range(groups - 1):
        extra_far_copy(d, peers[d]).wait_recv()
    total = extra_far[0]
    for p in range(1, groups):
        total = total + extra_far[p]
    extra_near[...] = total
    mine = pl.ds(pl.multiple_of(core * half, half), half)
    other = pl.ds(pl.multiple_of((1 - core) * half, half), half)
    goff[mine, :] = total[layers : layers + half]
    goff_remote = pltpu.make_async_remote_copy(
        src_ref=goff.at[mine],
        dst_ref=goff.at[mine],
        send_sem=new_send.at[chunks],
        recv_sem=new_recv.at[chunks],
        device_id=partner,
        device_id_type=MESH,
    )
    goff_remote.start()

    def new_copy(j):
        layer = CORES * j + core
        return pltpu.make_async_remote_copy(
            src_ref=new.at[layer],
            dst_ref=new.at[layer],
            send_sem=new_send.at[j],
            recv_sem=new_recv.at[j],
            device_id=partner,
            device_id_type=MESH,
        )

    def new_arrival(j):
        layer = CORES * j + 1 - core
        return pltpu.make_async_remote_copy(
            src_ref=new.at[layer],
            dst_ref=new.at[layer],
            send_sem=new_send.at[j],
            recv_sem=new_recv.at[j],
            device_id=partner,
            device_id_type=MESH,
        )

    def update(j, carry):
        for copy in far_arrivals(j):
            copy.wait_recv()
        total = far[0, j]
        for p in range(1, groups):
            total = total + far[p, j]
        total = total + jnp.where(first_row, extra_near[pl.ds(j, 1), :], 0.0)
        total = total + jnp.where(last_row, extra_near[pl.ds(chunks + j, 1), :], 0.0)
        layer = CORES * j + core
        new[layer] = cond[layer] * jnp.exp(-RATE * jnp.tanh(total))
        new_copy(j).start()
        return carry

    lax.fori_loop(0, chunks, update, 0)

    def drain(j, carry):
        near_copy(j).wait_send()
        for copy in far_copies(j):
            copy.wait_send()
        new_copy(j).wait_send()
        new_arrival(j).wait_recv()
        return carry

    @pl.when(has_behind)
    def _():
        to_behind.wait_send()

    @pl.when(has_ahead)
    def _():
        to_ahead.wait_send()

    extra_near_copy.wait_send()
    for d in range(groups - 1):
        extra_far_copy(d, group).wait_send()
    lax.fori_loop(0, chunks, drain, 0)
    goff_remote.wait_send()
    pltpu.make_async_remote_copy(
        src_ref=goff.at[other],
        dst_ref=goff.at[other],
        send_sem=new_send.at[chunks],
        recv_sem=new_recv.at[chunks],
        device_id=partner,
        device_id_type=MESH,
    ).wait_recv()


def write_out(*refs):
    sources, targets, sem = refs[:4], refs[4:8], refs[8]
    copies = [
        pltpu.make_async_copy(src, dst, sem.at[i])
        for i, (src, dst) in enumerate(zip(sources, targets))
    ]
    for copy in copies:
        copy.start()
    for copy in copies:
        copy.wait()


def solution(mesh):
    n_space, n_member = mesh.shape["space"], mesh.shape["member"]
    groups = n_member // CORES

    def body(
        start_temp,
        cotangent,
        conductivity,
        porosity,
        surface_temp,
        surface_offset,
        basal_flux,
        thickness,
        tile_len,
    ):
        layers, rows, across = conductivity.shape
        chunks = layers // CORES
        half = rows // CORES
        extra = layers + half
        f32 = jnp.float32
        whole = (layers, rows, across)
        plane = (rows, across)
        dma = pltpu.SemaphoreType.DMA

        def vmem(*shape):
            return pltpu.VMEM(shape, f32)

        hbm = pl.BlockSpec(memory_space=pltpu.HBM)
        cells = layers * rows * across
        heated, adj, new, goff = pl.pallas_call(
            lambda *refs: kernel(n_space, groups, *refs),
            out_shape=[pltpu.VMEM(s, f32) for s in (whole, whole, whole, plane)],
            in_specs=[pl.BlockSpec(memory_space=pltpu.SMEM)] + [hbm] * 8,
            out_specs=[pl.BlockSpec(memory_space=pltpu.VMEM)] * 4,
            scratch_shapes=[vmem(*whole)] * 4
            + [vmem(*plane)] * 5
            + [vmem(*whole)] * 4
            + [
                vmem(chunks, *plane),
                vmem(groups, chunks, *plane),
                vmem(2, 4, layers, across),
                vmem(2, 3, layers, across),
                vmem(2, 2, layers, across),
                vmem(CORES, extra, across),
                vmem(extra, across),
                vmem(groups, extra, across),
                vmem(*plane),
                dma((3, 8)),
                dma((2,)),
                dma((2,)),
                dma((chunks + 1,)),
                dma((chunks + 1,)),
                dma((max(groups - 1, 1), chunks + 1)),
                dma((groups, chunks + 1)),
                dma((chunks + 1,)),
                dma((chunks + 1,)),
            ],
            compiler_params=pltpu.CompilerParams(
                collective_id=0, has_side_effects=True, vmem_limit_bytes=48 * 1024 * 1024
            ),
            cost_estimate=pl.CostEstimate(
                flops=100 * cells, bytes_accessed=28 * cells, transcendentals=3 * cells
            ),
            name="heat_step",
        )(
            tile_len,
            *[
                pltpu.with_memory_space_constraint(x, pltpu.HBM)
                for x in (
                    start_temp[0],
                    porosity,
                    cotangent[0],
                    conductivity,
                    surface_temp[0],
                    surface_offset,
                    basal_flux,
                    thickness,
                )
            ]
        )
        heated, adj, new, goff = pl.pallas_call(
            write_out,
            out_shape=[pltpu.HBM(s, f32) for s in (whole, whole, whole, plane)],
            in_specs=[pl.BlockSpec(memory_space=pltpu.VMEM)] * 4,
            out_specs=[hbm] * 4,
            scratch_shapes=[dma((4,))],
            cost_estimate=pl.CostEstimate(flops=0, bytes_accessed=24 * cells, transcendentals=0),
            name="write_out",
        )(*[pltpu.with_memory_space_constraint(x, pltpu.VMEM) for x in (heated, adj, new, goff)])
        return heated[None], adj[None], new, goff

    in_specs = (
        P("member", None, "space", None),
        P("member", None, "space", None),
        P(None, "space", None),
        P(None, "space", None),
        P("member", "space", None),
        P("space", None),
        P("space", None),
        P("space", None),
        P("space"),
    )
    out_specs = (
        P("member", None, "space", None),
        P("member", None, "space", None),
        P(None, "space", None),
        P("space", None),
    )
    return jax.shard_map(body, mesh=mesh, in_specs=in_specs, out_specs=out_specs, check_vma=False)
```

```python
import jax
import jax.numpy as jnp
from jax import lax
from jax.experimental import pallas as pl
from jax.experimental.pallas import tpu as pltpu
from jax.sharding import PartitionSpec as P

STEP = 0.03
RATE = 0.5
MESH = pl.DeviceIdType.MESH
CORES = 2


def kernel(
    n_space,
    groups,
    len_ref,
    temp_hbm,
    por_hbm,
    cot_hbm,
    cond_hbm,
    surf_hbm,
    offset_hbm,
    basal_hbm,
    thick_hbm,
    heated,
    adj,
    new,
    goff,
    temp,
    por,
    cot,
    cond,
    surf,
    offset,
    basal,
    thick,
    inverse,
    weight,
    recip,
    slope,
    grad,
    near,
    far,
    edge_out,
    edge_in,
    edge,
    extra_out,
    extra_near,
    extra_far,
    goff_mine,
    in_sem,
    halo_send,
    halo_recv,
    near_send,
    near_recv,
    far_send,
    far_recv,
    new_send,
    new_recv,
):
    layers, rows, across = temp.shape
    chunks = layers // CORES
    half = rows // CORES
    space = lax.axis_index("space")
    member = lax.axis_index("member")
    core = lax.rem(member, CORES)
    group = lax.div(member, CORES)
    partner = (space, member + 1 - 2 * core)
    peers = [lax.rem(group + d, groups) for d in range(1, groups)]
    peer_ids = [(space, p * CORES + core) for p in peers]
    behind = (space - 1, member)
    ahead = (space + 1, member)
    has_behind = space > 0
    has_ahead = space < n_space - 1

    barrier = pltpu.get_barrier_semaphore()
    for other in [partner] + peer_ids:
        pl.semaphore_signal(barrier, inc=1, device_id=other, device_id_type=MESH)

    @pl.when(has_behind)
    def _():
        pl.semaphore_signal(barrier, inc=1, device_id=behind, device_id_type=MESH)

    @pl.when(has_ahead)
    def _():
        pl.semaphore_signal(barrier, inc=1, device_id=ahead, device_id_type=MESH)

    cuts = [0, 2 * CORES, 4 * CORES, layers]
    fields = [(temp_hbm, temp), (por_hbm, por), (cot_hbm, cot), (cond_hbm, cond)]
    planes = [(thick_hbm, thick), (surf_hbm, surf), (offset_hbm, offset), (basal_hbm, basal)]
    parts = [
        [(src.at[lo:hi], dst.at[lo:hi]) for src, dst in fields] for lo, hi in zip(cuts, cuts[1:])
    ]
    parts[0] += planes
    loads = [
        [pltpu.make_async_copy(src, dst, in_sem.at[p, i]) for i, (src, dst) in enumerate(part)]
        for p, part in enumerate(parts)
    ]
    for part in loads:
        for load in part:
            load.start()

    @pl.when(jnp.logical_not(has_behind))
    def _():
        edge_in[0] = jnp.zeros(edge_in.shape[1:], jnp.float32)

    @pl.when(jnp.logical_not(has_ahead))
    def _():
        edge_in[1] = jnp.zeros(edge_in.shape[1:], jnp.float32)

    for load in loads[0]:
        load.wait()
    count = len_ref[0]
    end = jnp.clip(count - 1, 0, rows - 1)
    row = lax.broadcasted_iota(jnp.int32, (rows, across), 0)
    col = lax.broadcasted_iota(jnp.int32, (rows, across), 1)
    live = row < count
    inner = (row >= 1) & live
    not_east = col < across - 1
    inverse[...] = 1.0 / (thick[...] * thick[...])

    def pointwise(v, p, c):
        th = jnp.tanh(v)
        q = p * (1.0 - th * th)
        r = 1.0 / (1.0 + 4.0 * q)
        return r, STEP * c * r, 8.0 * th * q

    to_behind = pltpu.make_async_remote_copy(
        src_ref=edge_out.at[0, 0:3],
        dst_ref=edge_in.at[1],
        send_sem=halo_send.at[0],
        recv_sem=halo_recv.at[1],
        device_id=behind,
        device_id_type=MESH,
    )
    to_ahead = pltpu.make_async_remote_copy(
        src_ref=edge_out.at[1, 0:3],
        dst_ref=edge_in.at[0],
        send_sem=halo_send.at[1],
        recv_sem=halo_recv.at[0],
        device_id=ahead,
        device_id_type=MESH,
    )

    def weigh(layer):
        r, w, s = pointwise(temp[layer], por[layer], cot[layer])
        w = jnp.where(live, w, 0.0)
        recip[layer] = r
        weight[layer] = w
        slope[layer] = w * r * s

    def lateral(layer):
        v, k, w = temp[layer], cond[layer], weight[layer]

        def east(x):
            return pltpu.roll(x, across - 1, 1)

        def west(x):
            return pltpu.roll(x, 1, 1)

        def prev(x):
            return pltpu.roll(x, 1, 0)

        def following(x):
            return pltpu.roll(x, rows - 1, 0)

        a = jnp.where(not_east, k + east(k), 0.0)
        dv = jnp.where(not_east, east(v) - v, 0.0)
        dw = east(w) - w
        f, b, g = a * dv, a * dw, dv * dw
        flow = f - west(f)
        back = b - west(b)
        cross = g + west(g)

        a = jnp.where(inner, k + prev(k), 0.0)
        dv = jnp.where(inner, prev(v) - v, 0.0)
        dw = prev(w) - w
        f, b, g = a * dv, a * dw, dv * dw
        flow = flow + (f - following(f))
        back = back + (b - following(b))
        cross = cross + (g + following(g))
        return flow, back, cross

    def face(layer):
        a = cond[layer] + cond[layer + 1]
        dv = temp[layer + 1] - temp[layer]
        dw = weight[layer + 1] - weight[layer]
        return a * dv, a * dw, dv * dw

    def store(layer, side, vertical):
        flow, back, cross = side
        f, b, g = vertical
        inv = inverse[...]
        heated[layer] = 0.5 * (flow + f * inv)
        adj[layer] = 0.5 * (back + b * inv)
        grad[layer] = -0.5 * (cross + g * inv)

    neighbours = has_behind.astype(jnp.int32) + has_ahead.astype(jnp.int32)

    def near_copy(j):
        return pltpu.make_async_remote_copy(
            src_ref=grad.at[CORES * j + 1 - core],
            dst_ref=near.at[j],
            send_sem=near_send.at[j],
            recv_sem=near_recv.at[j],
            device_id=partner,
            device_id_type=MESH,
        )

    def far_copies(j):
        return [
            pltpu.make_async_remote_copy(
                src_ref=far.at[group, j],
                dst_ref=far.at[group, j],
                send_sem=far_send.at[d, j],
                recv_sem=far_recv.at[group, j],
                device_id=peer_ids[d],
                device_id_type=MESH,
            )
            for d in range(groups - 1)
        ]

    def far_arrivals(j):
        return [
            pltpu.make_async_remote_copy(
                src_ref=far.at[peers[d], j],
                dst_ref=far.at[peers[d], j],
                send_sem=far_send.at[d, j],
                recv_sem=far_recv.at[peers[d], j],
                device_id=peer_ids[d],
                device_id_type=MESH,
            )
            for d in range(groups - 1)
        ]

    def chunk(j, first=False, last=False):
        layer = CORES * j
        if not last:
            weigh(layer + 2)
        middle_face = face(layer)
        f, b, g = middle_face
        if first:
            v, k, w = temp[layer], cond[layer], weight[layer]
            dv = surf[...] + offset[...] - v
            f = f + 4.0 * (k * dv)
            b = b - 4.0 * (k * w)
            g = g - 4.0 * (dv * w)
            goff_mine[...] = 2.0 * (k * inverse[...] * w)
        else:
            upper = face(layer - 1)
            f, b, g = f - upper[0], b - upper[1], g + upper[2]
        store(layer, lateral(layer), (f, b, g))
        f, b, g = middle_face
        f, b = -f, -b
        if not last:
            lower = face(layer + 1)
            f, b, g = f + lower[0], b + lower[1], g + lower[2]
        store(layer + 1, lateral(layer + 1), (f, b, g))
        if last:
            heated[layer + 1] += basal[...] / thick[...]
        if first:
            pl.semaphore_wait(barrier, groups + neighbours)
        near_copy(j).start()
        if not last:
            weigh(layer + 3)

    def pass_on(j):
        near_copy(j).wait_recv()
        far[group, j] = grad[CORES * j + core] + near[j]
        for copy in far_copies(j):
            copy.start()

    def step(j, carry):
        chunk(j)

        @pl.when(j > 2)
        def _():
            pass_on(j - 1)

        return carry

    extra_near_copy = pltpu.make_async_remote_copy(
        src_ref=extra_out.at[1 - core],
        dst_ref=extra_near,
        send_sem=near_send.at[chunks],
        recv_sem=near_recv.at[chunks],
        device_id=partner,
        device_id_type=MESH,
    )

    def extra_far_copy(d, slot):
        return pltpu.make_async_remote_copy(
            src_ref=extra_far.at[slot],
            dst_ref=extra_far.at[slot],
            send_sem=far_send.at[d, chunks],
            recv_sem=far_recv.at[slot, chunks],
            device_id=peer_ids[d],
            device_id_type=MESH,
        )

    weigh(0)
    weigh(1)
    chunk(0, first=True)
    for load in loads[1]:
        load.wait()
    chunk(1)
    pass_on(0)
    for load in loads[2]:
        load.wait()

    for layer in range(layers):
        at = pl.ds(layer, 1)
        for f, field in enumerate((temp, cond, cot, por)):
            edge_out[0, f, at, :] = field[layer, 0:1, :]
            edge_out[1, f, at, :] = field[layer, pl.ds(end, 1), :]
    for side in range(2):
        _, w, _ = pointwise(edge_out[side, 0], edge_out[side, 3], edge_out[side, 2])
        edge_out[side, 2] = w

    @pl.when(has_behind)
    def _():
        to_behind.start()

    @pl.when(has_ahead)
    def _():
        to_ahead.start()

    pass_on(1)
    middle = chunks // 2
    lax.fori_loop(2, middle, step, 0)

    @pl.when(has_ahead)
    def _():
        to_behind.wait_recv()

    @pl.when(has_behind)
    def _():
        to_ahead.wait_recv()

    for side in range(2):
        a = 0.5 * (edge_out[side, 1] + edge_in[side, 1])
        dv = edge_in[side, 0] - edge_out[side, 0]
        dw = edge_in[side, 2] - edge_out[side, 2]
        edge[side, 0] = a * dv
        edge[side, 1] = a * dw
        g = -0.5 * (dv * dw)
        for layer in range(layers):
            at = side * chunks + layer // CORES
            extra_out[layer % CORES, at : at + 1, :] = g[layer : layer + 1, :]
    for h in range(CORES):
        extra_out[h, layers : layers + half, :] = goff_mine[h * half : (h + 1) * half, :]
    extra_near_copy.start()

    lax.fori_loop(middle, chunks - 1, step, 0)
    extra_near_copy.wait_recv()
    extra_far[group] = extra_out[core] + extra_near[...]
    for d in range(groups - 1):
        extra_far_copy(d, group).start()
    chunk(chunks - 1, last=True)

    first_row = row == 0
    last_row = row == count - 1

    def finish(layer, carry):
        at = pl.ds(layer, 1)

        def edges(f):
            return jnp.where(first_row, edge[0, f, at, :], 0.0) + jnp.where(
                last_row, edge[1, f, at, :], 0.0
            )

        flow = heated[layer] + edges(0)
        heated[layer] = jnp.where(live, temp[layer] + STEP * (flow * recip[layer]), 0.0)
        adj[layer] = jnp.where(
            live, cot[layer] + (adj[layer] + edges(1) + slope[layer] * flow), 0.0
        )
        return carry

    pass_on(chunks - 2)
    lax.fori_loop(0, 4, finish, 0)
    pass_on(chunks - 1)
    lax.fori_loop(4, layers, finish, 0)

    for d in range(groups - 1):
        extra_far_copy(d, peers[d]).wait_recv()
    total = extra_far[0]
    for p in range(1, groups):
        total = total + extra_far[p]
    extra_near[...] = total
    mine = pl.ds(pl.multiple_of(core * half, half), half)
    other = pl.ds(pl.multiple_of((1 - core) * half, half), half)
    goff[mine, :] = total[layers : layers + half]
    goff_remote = pltpu.make_async_remote_copy(
        src_ref=goff.at[mine],
        dst_ref=goff.at[mine],
        send_sem=new_send.at[chunks],
        recv_sem=new_recv.at[chunks],
        device_id=partner,
        device_id_type=MESH,
    )
    goff_remote.start()

    def new_copy(j):
        layer = CORES * j + core
        return pltpu.make_async_remote_copy(
            src_ref=new.at[layer],
            dst_ref=new.at[layer],
            send_sem=new_send.at[j],
            recv_sem=new_recv.at[j],
            device_id=partner,
            device_id_type=MESH,
        )

    def new_arrival(j):
        layer = CORES * j + 1 - core
        return pltpu.make_async_remote_copy(
            src_ref=new.at[layer],
            dst_ref=new.at[layer],
            send_sem=new_send.at[j],
            recv_sem=new_recv.at[j],
            device_id=partner,
            device_id_type=MESH,
        )

    def update(j, carry):
        for copy in far_arrivals(j):
            copy.wait_recv()
        total = far[0, j]
        for p in range(1, groups):
            total = total + far[p, j]
        total = total + jnp.where(first_row, extra_near[pl.ds(j, 1), :], 0.0)
        total = total + jnp.where(last_row, extra_near[pl.ds(chunks + j, 1), :], 0.0)
        layer = CORES * j + core
        new[layer] = cond[layer] * jnp.exp(-RATE * jnp.tanh(total))
        new_copy(j).start()
        return carry

    lax.fori_loop(0, chunks, update, 0)

    def drain(j, carry):
        near_copy(j).wait_send()
        for copy in far_copies(j):
            copy.wait_send()
        new_copy(j).wait_send()
        new_arrival(j).wait_recv()
        return carry

    @pl.when(has_behind)
    def _():
        to_behind.wait_send()

    @pl.when(has_ahead)
    def _():
        to_ahead.wait_send()

    extra_near_copy.wait_send()
    for d in range(groups - 1):
        extra_far_copy(d, group).wait_send()
    lax.fori_loop(0, chunks, drain, 0)
    goff_remote.wait_send()
    pltpu.make_async_remote_copy(
        src_ref=goff.at[other],
        dst_ref=goff.at[other],
        send_sem=new_send.at[chunks],
        recv_sem=new_recv.at[chunks],
        device_id=partner,
        device_id_type=MESH,
    ).wait_recv()


def write_out(*refs):
    sources, targets, sem = refs[:4], refs[4:8], refs[8]
    copies = [
        pltpu.make_async_copy(src, dst, sem.at[i])
        for i, (src, dst) in enumerate(zip(sources, targets))
    ]
    for copy in copies:
        copy.start()
    for copy in copies:
        copy.wait()


def solution(mesh):
    n_space, n_member = mesh.shape["space"], mesh.shape["member"]
    groups = n_member // CORES

    def body(
        start_temp,
        cotangent,
        conductivity,
        porosity,
        surface_temp,
        surface_offset,
        basal_flux,
        thickness,
        tile_len,
    ):
        layers, rows, across = conductivity.shape
        chunks = layers // CORES
        half = rows // CORES
        extra = layers + half
        f32 = jnp.float32
        whole = (layers, rows, across)
        plane = (rows, across)
        dma = pltpu.SemaphoreType.DMA

        def vmem(*shape):
            return pltpu.VMEM(shape, f32)

        hbm = pl.BlockSpec(memory_space=pltpu.HBM)
        cells = layers * rows * across
        heated, adj, new, goff = pl.pallas_call(
            lambda *refs: kernel(n_space, groups, *refs),
            out_shape=[pltpu.VMEM(s, f32) for s in (whole, whole, whole, plane)],
            in_specs=[pl.BlockSpec(memory_space=pltpu.SMEM)] + [hbm] * 8,
            out_specs=[pl.BlockSpec(memory_space=pltpu.VMEM)] * 4,
            scratch_shapes=[vmem(*whole)] * 4
            + [vmem(*plane)] * 5
            + [vmem(*whole)] * 4
            + [
                vmem(chunks, *plane),
                vmem(groups, chunks, *plane),
                vmem(2, 4, layers, across),
                vmem(2, 3, layers, across),
                vmem(2, 2, layers, across),
                vmem(CORES, extra, across),
                vmem(extra, across),
                vmem(groups, extra, across),
                vmem(*plane),
                dma((3, 8)),
                dma((2,)),
                dma((2,)),
                dma((chunks + 1,)),
                dma((chunks + 1,)),
                dma((max(groups - 1, 1), chunks + 1)),
                dma((groups, chunks + 1)),
                dma((chunks + 1,)),
                dma((chunks + 1,)),
            ],
            compiler_params=pltpu.CompilerParams(
                collective_id=0, has_side_effects=True, vmem_limit_bytes=48 * 1024 * 1024
            ),
            cost_estimate=pl.CostEstimate(
                flops=100 * cells, bytes_accessed=28 * cells, transcendentals=3 * cells
            ),
            name="heat_step",
        )(
            tile_len,
            *[
                pltpu.with_memory_space_constraint(x, pltpu.HBM)
                for x in (
                    start_temp[0],
                    porosity,
                    cotangent[0],
                    conductivity,
                    surface_temp[0],
                    surface_offset,
                    basal_flux,
                    thickness,
                )
            ]
        )
        heated, adj, new, goff = pl.pallas_call(
            write_out,
            out_shape=[pltpu.HBM(s, f32) for s in (whole, whole, whole, plane)],
            in_specs=[pl.BlockSpec(memory_space=pltpu.VMEM)] * 4,
            out_specs=[hbm] * 4,
            scratch_shapes=[dma((4,))],
            cost_estimate=pl.CostEstimate(flops=0, bytes_accessed=24 * cells, transcendentals=0),
            name="write_out",
        )(*[pltpu.with_memory_space_constraint(x, pltpu.VMEM) for x in (heated, adj, new, goff)])
        return heated[None], adj[None], new, goff

    in_specs = (
        P("member", None, "space", None),
        P("member", None, "space", None),
        P(None, "space", None),
        P(None, "space", None),
        P("member", "space", None),
        P("space", None),
        P("space", None),
        P("space", None),
        P("space"),
    )
    out_specs = (
        P("member", None, "space", None),
        P("member", None, "space", None),
        P(None, "space", None),
        P("space", None),
    )
    return jax.shard_map(body, mesh=mesh, in_specs=in_specs, out_specs=out_specs, check_vma=False)
```

```python
import jax
import jax.numpy as jnp
from jax import lax
from jax.experimental import pallas as pl
from jax.experimental.pallas import tpu as pltpu
from jax.sharding import PartitionSpec as P

STEP = 0.03
RATE = 0.5
MESH = pl.DeviceIdType.MESH
CORES = 2


def kernel(
    n_space,
    groups,
    len_ref,
    temp_hbm,
    por_hbm,
    cot_hbm,
    cond_hbm,
    surf_hbm,
    offset_hbm,
    basal_hbm,
    thick_hbm,
    heated,
    adj,
    new,
    goff,
    temp,
    por,
    cot,
    cond,
    surf,
    offset,
    basal,
    thick,
    inverse,
    weight,
    recip,
    slope,
    grad,
    near,
    far,
    edge_out,
    edge_in,
    edge,
    extra_out,
    extra_near,
    extra_far,
    goff_mine,
    in_sem,
    halo_send,
    halo_recv,
    near_send,
    near_recv,
    far_send,
    far_recv,
    new_send,
    new_recv,
):
    layers, rows, across = temp.shape
    chunks = layers // CORES
    half = rows // CORES
    space = lax.axis_index("space")
    member = lax.axis_index("member")
    core = lax.rem(member, CORES)
    group = lax.div(member, CORES)
    partner = (space, member + 1 - 2 * core)
    peers = [lax.rem(group + d, groups) for d in range(1, groups)]
    peer_ids = [(space, p * CORES + core) for p in peers]
    behind = (space - 1, member)
    ahead = (space + 1, member)
    has_behind = space > 0
    has_ahead = space < n_space - 1

    barrier = pltpu.get_barrier_semaphore()
    for other in [partner] + peer_ids:
        pl.semaphore_signal(barrier, inc=1, device_id=other, device_id_type=MESH)

    @pl.when(has_behind)
    def _():
        pl.semaphore_signal(barrier, inc=1, device_id=behind, device_id_type=MESH)

    @pl.when(has_ahead)
    def _():
        pl.semaphore_signal(barrier, inc=1, device_id=ahead, device_id_type=MESH)

    cuts = [0, 2 * CORES, 4 * CORES, layers]
    fields = [(temp_hbm, temp), (por_hbm, por), (cot_hbm, cot), (cond_hbm, cond)]
    planes = [(thick_hbm, thick), (surf_hbm, surf), (offset_hbm, offset), (basal_hbm, basal)]
    parts = [
        [(src.at[lo:hi], dst.at[lo:hi]) for src, dst in fields] for lo, hi in zip(cuts, cuts[1:])
    ]
    parts[0] += planes
    loads = [
        [pltpu.make_async_copy(src, dst, in_sem.at[p, i]) for i, (src, dst) in enumerate(part)]
        for p, part in enumerate(parts)
    ]
    for part in loads:
        for load in part:
            load.start()

    @pl.when(jnp.logical_not(has_behind))
    def _():
        edge_in[0] = jnp.zeros(edge_in.shape[1:], jnp.float32)

    @pl.when(jnp.logical_not(has_ahead))
    def _():
        edge_in[1] = jnp.zeros(edge_in.shape[1:], jnp.float32)

    for load in loads[0]:
        load.wait()
    count = len_ref[0]
    end = jnp.clip(count - 1, 0, rows - 1)
    row = lax.broadcasted_iota(jnp.int32, (rows, across), 0)
    col = lax.broadcasted_iota(jnp.int32, (rows, across), 1)
    live = row < count
    inner = (row >= 1) & live
    not_east = col < across - 1
    inverse[...] = 1.0 / (thick[...] * thick[...])

    def pointwise(v, p, c):
        th = jnp.tanh(v)
        q = p * (1.0 - th * th)
        r = 1.0 / (1.0 + 4.0 * q)
        return r, STEP * c * r, 8.0 * th * q

    to_behind = pltpu.make_async_remote_copy(
        src_ref=edge_out.at[0, 0:3],
        dst_ref=edge_in.at[1],
        send_sem=halo_send.at[0],
        recv_sem=halo_recv.at[1],
        device_id=behind,
        device_id_type=MESH,
    )
    to_ahead = pltpu.make_async_remote_copy(
        src_ref=edge_out.at[1, 0:3],
        dst_ref=edge_in.at[0],
        send_sem=halo_send.at[1],
        recv_sem=halo_recv.at[0],
        device_id=ahead,
        device_id_type=MESH,
    )

    def weigh(layer):
        r, w, s = pointwise(temp[layer], por[layer], cot[layer])
        w = jnp.where(live, w, 0.0)
        recip[layer] = r
        weight[layer] = w
        slope[layer] = w * r * s

    def lateral(layer):
        v, k, w = temp[layer], cond[layer], weight[layer]

        def east(x):
            return pltpu.roll(x, across - 1, 1)

        def west(x):
            return pltpu.roll(x, 1, 1)

        def prev(x):
            return pltpu.roll(x, 1, 0)

        def following(x):
            return pltpu.roll(x, rows - 1, 0)

        a = jnp.where(not_east, k + east(k), 0.0)
        dv = jnp.where(not_east, east(v) - v, 0.0)
        dw = east(w) - w
        f, b, g = a * dv, a * dw, dv * dw
        flow = f - west(f)
        back = b - west(b)
        cross = g + west(g)

        a = jnp.where(inner, k + prev(k), 0.0)
        dv = jnp.where(inner, prev(v) - v, 0.0)
        dw = prev(w) - w
        f, b, g = a * dv, a * dw, dv * dw
        flow = flow + (f - following(f))
        back = back + (b - following(b))
        cross = cross + (g + following(g))
        return flow, back, cross

    def face(layer):
        a = cond[layer] + cond[layer + 1]
        dv = temp[layer + 1] - temp[layer]
        dw = weight[layer + 1] - weight[layer]
        return a * dv, a * dw, dv * dw

    def store(layer, side, vertical):
        flow, back, cross = side
        f, b, g = vertical
        inv = inverse[...]
        heated[layer] = 0.5 * (flow + f * inv)
        adj[layer] = 0.5 * (back + b * inv)
        grad[layer] = -0.5 * (cross + g * inv)

    neighbours = has_behind.astype(jnp.int32) + has_ahead.astype(jnp.int32)

    def near_copy(j):
        return pltpu.make_async_remote_copy(
            src_ref=grad.at[CORES * j + 1 - core],
            dst_ref=near.at[j],
            send_sem=near_send.at[j],
            recv_sem=near_recv.at[j],
            device_id=partner,
            device_id_type=MESH,
        )

    def far_copies(j):
        return [
            pltpu.make_async_remote_copy(
                src_ref=far.at[group, j],
                dst_ref=far.at[group, j],
                send_sem=far_send.at[d, j],
                recv_sem=far_recv.at[group, j],
                device_id=peer_ids[d],
                device_id_type=MESH,
            )
            for d in range(groups - 1)
        ]

    def far_arrivals(j):
        return [
            pltpu.make_async_remote_copy(
                src_ref=far.at[peers[d], j],
                dst_ref=far.at[peers[d], j],
                send_sem=far_send.at[d, j],
                recv_sem=far_recv.at[peers[d], j],
                device_id=peer_ids[d],
                device_id_type=MESH,
            )
            for d in range(groups - 1)
        ]

    def chunk(j, first=False, last=False):
        layer = CORES * j
        if not last:
            weigh(layer + 2)
        middle_face = face(layer)
        f, b, g = middle_face
        if first:
            v, k, w = temp[layer], cond[layer], weight[layer]
            dv = surf[...] + offset[...] - v
            f = f + 4.0 * (k * dv)
            b = b - 4.0 * (k * w)
            g = g - 4.0 * (dv * w)
            goff_mine[...] = 2.0 * (k * inverse[...] * w)
        else:
            upper = face(layer - 1)
            f, b, g = f - upper[0], b - upper[1], g + upper[2]
        store(layer, lateral(layer), (f, b, g))
        if not isinstance(j, int):

            @pl.when(j > 3)
            def _():
                pass_on(j - 2)

        elif j > 3:
            pass_on(j - 2)
        f, b, g = middle_face
        f, b = -f, -b
        if not last:
            lower = face(layer + 1)
            f, b, g = f + lower[0], b + lower[1], g + lower[2]
        store(layer + 1, lateral(layer + 1), (f, b, g))
        if last:
            heated[layer + 1] += basal[...] / thick[...]
        if first:
            pl.semaphore_wait(barrier, groups + neighbours)
        near_copy(j).start()
        if not last:
            weigh(layer + 3)

    def pass_on(j):
        near_copy(j).wait_recv()
        far[group, j] = grad[CORES * j + core] + near[j]
        for copy in far_copies(j):
            copy.start()

    def step(j, carry):
        chunk(j)
        return carry

    extra_near_copy = pltpu.make_async_remote_copy(
        src_ref=extra_out.at[1 - core],
        dst_ref=extra_near,
        send_sem=near_send.at[chunks],
        recv_sem=near_recv.at[chunks],
        device_id=partner,
        device_id_type=MESH,
    )

    def extra_far_copy(d, slot):
        return pltpu.make_async_remote_copy(
            src_ref=extra_far.at[slot],
            dst_ref=extra_far.at[slot],
            send_sem=far_send.at[d, chunks],
            recv_sem=far_recv.at[slot, chunks],
            device_id=peer_ids[d],
            device_id_type=MESH,
        )

    weigh(0)
    weigh(1)
    chunk(0, first=True)
    for load in loads[1]:
        load.wait()
    chunk(1)
    pass_on(0)
    for load in loads[2]:
        load.wait()

    for layer in range(layers):
        at = pl.ds(layer, 1)
        for f, field in enumerate((temp, cond, cot, por)):
            edge_out[0, f, at, :] = field[layer, 0:1, :]
            edge_out[1, f, at, :] = field[layer, pl.ds(end, 1), :]
    for side in range(2):
        _, w, _ = pointwise(edge_out[side, 0], edge_out[side, 3], edge_out[side, 2])
        edge_out[side, 2] = w

    @pl.when(has_behind)
    def _():
        to_behind.start()

    @pl.when(has_ahead)
    def _():
        to_ahead.start()

    pass_on(1)
    lax.fori_loop(2, chunks - 1, step, 0)
    chunk(chunks - 1, last=True)
    pass_on(chunks - 2)

    @pl.when(has_ahead)
    def _():
        to_behind.wait_recv()

    @pl.when(has_behind)
    def _():
        to_ahead.wait_recv()

    for side in range(2):
        a = 0.5 * (edge_out[side, 1] + edge_in[side, 1])
        dv = edge_in[side, 0] - edge_out[side, 0]
        dw = edge_in[side, 2] - edge_out[side, 2]
        edge[side, 0] = a * dv
        edge[side, 1] = a * dw
        g = -0.5 * (dv * dw)
        for layer in range(layers):
            at = side * chunks + layer // CORES
            extra_out[layer % CORES, at : at + 1, :] = g[layer : layer + 1, :]
    for h in range(CORES):
        extra_out[h, layers : layers + half, :] = goff_mine[h * half : (h + 1) * half, :]
    extra_near_copy.start()

    first_row = row == 0
    last_row = row == count - 1

    def finish(layer, carry):
        at = pl.ds(layer, 1)

        def edges(f):
            return jnp.where(first_row, edge[0, f, at, :], 0.0) + jnp.where(
                last_row, edge[1, f, at, :], 0.0
            )

        flow = heated[layer] + edges(0)
        heated[layer] = jnp.where(live, temp[layer] + STEP * (flow * recip[layer]), 0.0)
        adj[layer] = jnp.where(
            live, cot[layer] + (adj[layer] + edges(1) + slope[layer] * flow), 0.0
        )
        return carry

    lax.fori_loop(0, 2, finish, 0)
    pass_on(chunks - 1)
    lax.fori_loop(2, 8, finish, 0)
    extra_near_copy.wait_recv()
    extra_far[group] = extra_out[core] + extra_near[...]
    for d in range(groups - 1):
        extra_far_copy(d, group).start()
    lax.fori_loop(8, layers, finish, 0)

    def sent(j, carry):
        near_copy(j).wait_send()
        return carry

    lax.fori_loop(0, chunks, sent, 0)
    extra_near_copy.wait_send()

    @pl.when(has_behind)
    def _():
        to_behind.wait_send()

    @pl.when(has_ahead)
    def _():
        to_ahead.wait_send()

    for d in range(groups - 1):
        extra_far_copy(d, peers[d]).wait_recv()
    total = extra_far[0]
    for p in range(1, groups):
        total = total + extra_far[p]
    extra_near[...] = total
    mine = pl.ds(pl.multiple_of(core * half, half), half)
    other = pl.ds(pl.multiple_of((1 - core) * half, half), half)
    goff[mine, :] = total[layers : layers + half]
    goff_remote = pltpu.make_async_remote_copy(
        src_ref=goff.at[mine],
        dst_ref=goff.at[mine],
        send_sem=new_send.at[chunks],
        recv_sem=new_recv.at[chunks],
        device_id=partner,
        device_id_type=MESH,
    )
    goff_remote.start()

    def new_copy(j):
        layer = CORES * j + core
        return pltpu.make_async_remote_copy(
            src_ref=new.at[layer],
            dst_ref=new.at[layer],
            send_sem=new_send.at[j],
            recv_sem=new_recv.at[j],
            device_id=partner,
            device_id_type=MESH,
        )

    def new_arrival(j):
        layer = CORES * j + 1 - core
        return pltpu.make_async_remote_copy(
            src_ref=new.at[layer],
            dst_ref=new.at[layer],
            send_sem=new_send.at[j],
            recv_sem=new_recv.at[j],
            device_id=partner,
            device_id_type=MESH,
        )

    def update(j, carry):
        for copy in far_arrivals(j):
            copy.wait_recv()
        total = far[0, j]
        for p in range(1, groups):
            total = total + far[p, j]
        total = total + jnp.where(first_row, extra_near[pl.ds(j, 1), :], 0.0)
        total = total + jnp.where(last_row, extra_near[pl.ds(chunks + j, 1), :], 0.0)
        layer = CORES * j + core
        new[layer] = cond[layer] * jnp.exp(-RATE * jnp.tanh(total))
        new_copy(j).start()
        for copy in far_copies(j):
            copy.wait_send()
        return carry

    lax.fori_loop(0, chunks, update, 0)

    def drain(j, carry):
        new_copy(j).wait_send()
        new_arrival(j).wait_recv()
        return carry

    for d in range(groups - 1):
        extra_far_copy(d, group).wait_send()
    lax.fori_loop(0, chunks, drain, 0)
    goff_remote.wait_send()
    pltpu.make_async_remote_copy(
        src_ref=goff.at[other],
        dst_ref=goff.at[other],
        send_sem=new_send.at[chunks],
        recv_sem=new_recv.at[chunks],
        device_id=partner,
        device_id_type=MESH,
    ).wait_recv()


def write_out(*refs):
    sources, targets, sem = refs[:4], refs[4:8], refs[8]
    copies = [
        pltpu.make_async_copy(src, dst, sem.at[i])
        for i, (src, dst) in enumerate(zip(sources, targets))
    ]
    for copy in copies:
        copy.start()
    for copy in copies:
        copy.wait()


def solution(mesh):
    n_space, n_member = mesh.shape["space"], mesh.shape["member"]
    groups = n_member // CORES

    def body(
        start_temp,
        cotangent,
        conductivity,
        porosity,
        surface_temp,
        surface_offset,
        basal_flux,
        thickness,
        tile_len,
    ):
        layers, rows, across = conductivity.shape
        chunks = layers // CORES
        half = rows // CORES
        extra = layers + half
        f32 = jnp.float32
        whole = (layers, rows, across)
        plane = (rows, across)
        dma = pltpu.SemaphoreType.DMA

        def vmem(*shape):
            return pltpu.VMEM(shape, f32)

        hbm = pl.BlockSpec(memory_space=pltpu.HBM)
        cells = layers * rows * across
        heated, adj, new, goff = pl.pallas_call(
            lambda *refs: kernel(n_space, groups, *refs),
            out_shape=[pltpu.VMEM(s, f32) for s in (whole, whole, whole, plane)],
            in_specs=[pl.BlockSpec(memory_space=pltpu.SMEM)] + [hbm] * 8,
            out_specs=[pl.BlockSpec(memory_space=pltpu.VMEM)] * 4,
            scratch_shapes=[vmem(*whole)] * 4
            + [vmem(*plane)] * 5
            + [vmem(*whole)] * 4
            + [
                vmem(chunks, *plane),
                vmem(groups, chunks, *plane),
                vmem(2, 4, layers, across),
                vmem(2, 3, layers, across),
                vmem(2, 2, layers, across),
                vmem(CORES, extra, across),
                vmem(extra, across),
                vmem(groups, extra, across),
                vmem(*plane),
                dma((3, 8)),
                dma((2,)),
                dma((2,)),
                dma((chunks + 1,)),
                dma((chunks + 1,)),
                dma((max(groups - 1, 1), chunks + 1)),
                dma((groups, chunks + 1)),
                dma((chunks + 1,)),
                dma((chunks + 1,)),
            ],
            compiler_params=pltpu.CompilerParams(
                collective_id=0, has_side_effects=True, vmem_limit_bytes=48 * 1024 * 1024
            ),
            cost_estimate=pl.CostEstimate(
                flops=100 * cells, bytes_accessed=28 * cells, transcendentals=3 * cells
            ),
            name="heat_step",
        )(
            tile_len,
            *[
                pltpu.with_memory_space_constraint(x, pltpu.HBM)
                for x in (
                    start_temp[0],
                    porosity,
                    cotangent[0],
                    conductivity,
                    surface_temp[0],
                    surface_offset,
                    basal_flux,
                    thickness,
                )
            ]
        )
        heated, adj, new, goff = pl.pallas_call(
            write_out,
            out_shape=[pltpu.HBM(s, f32) for s in (whole, whole, whole, plane)],
            in_specs=[pl.BlockSpec(memory_space=pltpu.VMEM)] * 4,
            out_specs=[hbm] * 4,
            scratch_shapes=[dma((4,))],
            cost_estimate=pl.CostEstimate(flops=0, bytes_accessed=24 * cells, transcendentals=0),
            name="write_out",
        )(*[pltpu.with_memory_space_constraint(x, pltpu.VMEM) for x in (heated, adj, new, goff)])
        return heated[None], adj[None], new, goff

    in_specs = (
        P("member", None, "space", None),
        P("member", None, "space", None),
        P(None, "space", None),
        P(None, "space", None),
        P("member", "space", None),
        P("space", None),
        P("space", None),
        P("space", None),
        P("space"),
    )
    out_specs = (
        P("member", None, "space", None),
        P("member", None, "space", None),
        P(None, "space", None),
        P("space", None),
    )
    return jax.shard_map(body, mesh=mesh, in_specs=in_specs, out_specs=out_specs, check_vma=False)
```

```python
import jax
import jax.numpy as jnp
from jax import lax
from jax.experimental import pallas as pl
from jax.experimental.pallas import tpu as pltpu
from jax.sharding import PartitionSpec as P

STEP = 0.03
RATE = 0.5
MESH = pl.DeviceIdType.MESH
CORES = 2


def kernel(
    n_space,
    groups,
    len_ref,
    temp_hbm,
    por_hbm,
    cot_hbm,
    cond_hbm,
    surf_hbm,
    offset_hbm,
    basal_hbm,
    thick_hbm,
    heated,
    adj,
    new,
    goff,
    temp,
    por,
    cot,
    cond,
    surf,
    offset,
    basal,
    thick,
    inverse,
    weight,
    recip,
    slope,
    grad,
    near,
    far,
    edge_out,
    edge_in,
    edge,
    extra_out,
    extra_near,
    extra_far,
    goff_mine,
    in_sem,
    halo_send,
    halo_recv,
    near_send,
    near_recv,
    far_send,
    far_recv,
    new_send,
    new_recv,
):
    layers, rows, across = temp.shape
    chunks = layers // CORES
    half = rows // CORES
    space = lax.axis_index("space")
    member = lax.axis_index("member")
    core = lax.rem(member, CORES)
    group = lax.div(member, CORES)
    partner = (space, member + 1 - 2 * core)
    peers = [lax.rem(group + d, groups) for d in range(1, groups)]
    peer_ids = [(space, p * CORES + core) for p in peers]
    behind = (space - 1, member)
    ahead = (space + 1, member)
    has_behind = space > 0
    has_ahead = space < n_space - 1

    barrier = pltpu.get_barrier_semaphore()
    for other in [partner] + peer_ids:
        pl.semaphore_signal(barrier, inc=1, device_id=other, device_id_type=MESH)

    @pl.when(has_behind)
    def _():
        pl.semaphore_signal(barrier, inc=1, device_id=behind, device_id_type=MESH)

    @pl.when(has_ahead)
    def _():
        pl.semaphore_signal(barrier, inc=1, device_id=ahead, device_id_type=MESH)

    cuts = [0, 2 * CORES, 4 * CORES, layers]
    fields = [(temp_hbm, temp), (por_hbm, por), (cot_hbm, cot), (cond_hbm, cond)]
    planes = [(thick_hbm, thick), (surf_hbm, surf), (offset_hbm, offset), (basal_hbm, basal)]
    parts = [
        [(src.at[lo:hi], dst.at[lo:hi]) for src, dst in fields] for lo, hi in zip(cuts, cuts[1:])
    ]
    parts[0] += planes
    loads = [
        [pltpu.make_async_copy(src, dst, in_sem.at[p, i]) for i, (src, dst) in enumerate(part)]
        for p, part in enumerate(parts)
    ]
    for part in loads:
        for load in part:
            load.start()

    @pl.when(jnp.logical_not(has_behind))
    def _():
        edge_in[0] = jnp.zeros(edge_in.shape[1:], jnp.float32)

    @pl.when(jnp.logical_not(has_ahead))
    def _():
        edge_in[1] = jnp.zeros(edge_in.shape[1:], jnp.float32)

    for load in loads[0]:
        load.wait()
    count = len_ref[0]
    end = jnp.clip(count - 1, 0, rows - 1)
    row = lax.broadcasted_iota(jnp.int32, (rows, across), 0)
    col = lax.broadcasted_iota(jnp.int32, (rows, across), 1)
    live = row < count
    inner = (row >= 1) & live
    not_east = col < across - 1
    inverse[...] = 1.0 / (thick[...] * thick[...])

    def pointwise(v, p, c):
        th = jnp.tanh(v)
        q = p * (1.0 - th * th)
        r = 1.0 / (1.0 + 4.0 * q)
        return r, STEP * c * r, 8.0 * th * q

    to_behind = pltpu.make_async_remote_copy(
        src_ref=edge_out.at[0, 0:3],
        dst_ref=edge_in.at[1],
        send_sem=halo_send.at[0],
        recv_sem=halo_recv.at[1],
        device_id=behind,
        device_id_type=MESH,
    )
    to_ahead = pltpu.make_async_remote_copy(
        src_ref=edge_out.at[1, 0:3],
        dst_ref=edge_in.at[0],
        send_sem=halo_send.at[1],
        recv_sem=halo_recv.at[0],
        device_id=ahead,
        device_id_type=MESH,
    )

    def weigh(layer):
        r, w, s = pointwise(temp[layer], por[layer], cot[layer])
        w = jnp.where(live, w, 0.0)
        recip[layer] = r
        weight[layer] = w
        slope[layer] = w * r * s

    def lateral(layer):
        v, k, w = temp[layer], cond[layer], weight[layer]

        def east(x):
            return pltpu.roll(x, across - 1, 1)

        def west(x):
            return pltpu.roll(x, 1, 1)

        def prev(x):
            return pltpu.roll(x, 1, 0)

        def following(x):
            return pltpu.roll(x, rows - 1, 0)

        a = jnp.where(not_east, k + east(k), 0.0)
        dv = jnp.where(not_east, east(v) - v, 0.0)
        dw = east(w) - w
        f, b, g = a * dv, a * dw, dv * dw
        flow = f - west(f)
        back = b - west(b)
        cross = g + west(g)

        a = jnp.where(inner, k + prev(k), 0.0)
        dv = jnp.where(inner, prev(v) - v, 0.0)
        dw = prev(w) - w
        f, b, g = a * dv, a * dw, dv * dw
        flow = flow + (f - following(f))
        back = back + (b - following(b))
        cross = cross + (g + following(g))
        return flow, back, cross

    def face(layer):
        a = cond[layer] + cond[layer + 1]
        dv = temp[layer + 1] - temp[layer]
        dw = weight[layer + 1] - weight[layer]
        return a * dv, a * dw, dv * dw

    def store(layer, side, vertical):
        flow, back, cross = side
        f, b, g = vertical
        inv = inverse[...]
        heated[layer] = 0.5 * (flow + f * inv)
        adj[layer] = 0.5 * (back + b * inv)
        grad[layer] = -0.5 * (cross + g * inv)

    neighbours = has_behind.astype(jnp.int32) + has_ahead.astype(jnp.int32)

    def near_copy(j):
        return pltpu.make_async_remote_copy(
            src_ref=grad.at[CORES * j + 1 - core],
            dst_ref=near.at[j],
            send_sem=near_send.at[j],
            recv_sem=near_recv.at[j],
            device_id=partner,
            device_id_type=MESH,
        )

    def far_copies(j):
        return [
            pltpu.make_async_remote_copy(
                src_ref=far.at[group, j],
                dst_ref=far.at[group, j],
                send_sem=far_send.at[d, j],
                recv_sem=far_recv.at[group, j],
                device_id=peer_ids[d],
                device_id_type=MESH,
            )
            for d in range(groups - 1)
        ]

    def far_arrivals(j):
        return [
            pltpu.make_async_remote_copy(
                src_ref=far.at[peers[d], j],
                dst_ref=far.at[peers[d], j],
                send_sem=far_send.at[d, j],
                recv_sem=far_recv.at[peers[d], j],
                device_id=peer_ids[d],
                device_id_type=MESH,
            )
            for d in range(groups - 1)
        ]

    def chunk(j, first=False, last=False):
        layer = CORES * j
        if not last:
            weigh(layer + 2)
        middle_face = face(layer)
        f, b, g = middle_face
        if first:
            v, k, w = temp[layer], cond[layer], weight[layer]
            dv = surf[...] + offset[...] - v
            f = f + 4.0 * (k * dv)
            b = b - 4.0 * (k * w)
            g = g - 4.0 * (dv * w)
            goff_mine[...] = 2.0 * (k * inverse[...] * w)
        else:
            upper = face(layer - 1)
            f, b, g = f - upper[0], b - upper[1], g + upper[2]
        store(layer, lateral(layer), (f, b, g))
        if not isinstance(j, int):

            @pl.when(j > 3)
            def _():
                pass_on(j - 2)

        elif j > 3:
            pass_on(j - 2)
        f, b, g = middle_face
        f, b = -f, -b
        if not last:
            lower = face(layer + 1)
            f, b, g = f + lower[0], b + lower[1], g + lower[2]
        store(layer + 1, lateral(layer + 1), (f, b, g))
        if last:
            heated[layer + 1] += basal[...] / thick[...]
        if first:
            pl.semaphore_wait(barrier, groups + neighbours)
        near_copy(j).start()
        if not last:
            weigh(layer + 3)

    def pass_on(j):
        near_copy(j).wait_recv()
        far[group, j] = grad[CORES * j + core] + near[j]
        for copy in far_copies(j):
            copy.start()

    def step(j, carry):
        chunk(j)

        @pl.when(j == 2)
        def _():
            pass_on(1)

        return carry

    extra_near_copy = pltpu.make_async_remote_copy(
        src_ref=extra_out.at[1 - core],
        dst_ref=extra_near,
        send_sem=near_send.at[chunks],
        recv_sem=near_recv.at[chunks],
        device_id=partner,
        device_id_type=MESH,
    )

    def extra_far_copy(d, slot):
        return pltpu.make_async_remote_copy(
            src_ref=extra_far.at[slot],
            dst_ref=extra_far.at[slot],
            send_sem=far_send.at[d, chunks],
            recv_sem=far_recv.at[slot, chunks],
            device_id=peer_ids[d],
            device_id_type=MESH,
        )

    weigh(0)
    weigh(1)
    chunk(0, first=True)
    for load in loads[1] + loads[2]:
        load.wait()

    for layer in range(layers):
        at = pl.ds(layer, 1)
        for f, field in enumerate((temp, cond, cot, por)):
            edge_out[0, f, at, :] = field[layer, 0:1, :]
            edge_out[1, f, at, :] = field[layer, pl.ds(end, 1), :]
    for side in range(2):
        _, w, _ = pointwise(edge_out[side, 0], edge_out[side, 3], edge_out[side, 2])
        edge_out[side, 2] = w

    @pl.when(has_behind)
    def _():
        to_behind.start()

    @pl.when(has_ahead)
    def _():
        to_ahead.start()

    pass_on(0)
    lax.fori_loop(1, chunks - 1, step, 0)

    @pl.when(has_ahead)
    def _():
        to_behind.wait_recv()

    @pl.when(has_behind)
    def _():
        to_ahead.wait_recv()

    for side in range(2):
        a = 0.5 * (edge_out[side, 1] + edge_in[side, 1])
        dv = edge_in[side, 0] - edge_out[side, 0]
        dw = edge_in[side, 2] - edge_out[side, 2]
        edge[side, 0] = a * dv
        edge[side, 1] = a * dw
        g = -0.5 * (dv * dw)
        for layer in range(layers):
            at = side * chunks + layer // CORES
            extra_out[layer % CORES, at : at + 1, :] = g[layer : layer + 1, :]
    for h in range(CORES):
        extra_out[h, layers : layers + half, :] = goff_mine[h * half : (h + 1) * half, :]
    extra_near_copy.start()
    chunk(chunks - 1, last=True)
    pass_on(chunks - 2)
    extra_near_copy.wait_recv()
    extra_far[group] = extra_out[core] + extra_near[...]
    for d in range(groups - 1):
        extra_far_copy(d, group).start()

    first_row = row == 0
    last_row = row == count - 1

    def finish(layer, carry):
        at = pl.ds(layer, 1)

        def edges(f):
            return jnp.where(first_row, edge[0, f, at, :], 0.0) + jnp.where(
                last_row, edge[1, f, at, :], 0.0
            )

        flow = heated[layer] + edges(0)
        heated[layer] = jnp.where(live, temp[layer] + STEP * (flow * recip[layer]), 0.0)
        adj[layer] = jnp.where(
            live, cot[layer] + (adj[layer] + edges(1) + slope[layer] * flow), 0.0
        )
        return carry

    lax.fori_loop(0, 2, finish, 0)
    pass_on(chunks - 1)
    lax.fori_loop(2, layers, finish, 0)

    def sent(j, carry):
        near_copy(j).wait_send()
        return carry

    lax.fori_loop(0, chunks, sent, 0)
    extra_near_copy.wait_send()

    @pl.when(has_behind)
    def _():
        to_behind.wait_send()

    @pl.when(has_ahead)
    def _():
        to_ahead.wait_send()

    for d in range(groups - 1):
        extra_far_copy(d, peers[d]).wait_recv()
    total = extra_far[0]
    for p in range(1, groups):
        total = total + extra_far[p]
    extra_near[...] = total
    mine = pl.ds(pl.multiple_of(core * half, half), half)
    other = pl.ds(pl.multiple_of((1 - core) * half, half), half)
    goff[mine, :] = total[layers : layers + half]
    goff_remote = pltpu.make_async_remote_copy(
        src_ref=goff.at[mine],
        dst_ref=goff.at[mine],
        send_sem=new_send.at[chunks],
        recv_sem=new_recv.at[chunks],
        device_id=partner,
        device_id_type=MESH,
    )
    goff_remote.start()

    def new_copy(j):
        layer = CORES * j + core
        return pltpu.make_async_remote_copy(
            src_ref=new.at[layer],
            dst_ref=new.at[layer],
            send_sem=new_send.at[j],
            recv_sem=new_recv.at[j],
            device_id=partner,
            device_id_type=MESH,
        )

    def new_arrival(j):
        layer = CORES * j + 1 - core
        return pltpu.make_async_remote_copy(
            src_ref=new.at[layer],
            dst_ref=new.at[layer],
            send_sem=new_send.at[j],
            recv_sem=new_recv.at[j],
            device_id=partner,
            device_id_type=MESH,
        )

    def update(j, carry):
        for copy in far_arrivals(j):
            copy.wait_recv()
        total = far[0, j]
        for p in range(1, groups):
            total = total + far[p, j]
        total = total + jnp.where(first_row, extra_near[pl.ds(j, 1), :], 0.0)
        total = total + jnp.where(last_row, extra_near[pl.ds(chunks + j, 1), :], 0.0)
        layer = CORES * j + core
        new[layer] = cond[layer] * jnp.exp(-RATE * jnp.tanh(total))
        new_copy(j).start()
        for copy in far_copies(j):
            copy.wait_send()
        return carry

    lax.fori_loop(0, chunks, update, 0)

    def drain(j, carry):
        new_copy(j).wait_send()
        new_arrival(j).wait_recv()
        return carry

    for d in range(groups - 1):
        extra_far_copy(d, group).wait_send()
    lax.fori_loop(0, chunks, drain, 0)
    goff_remote.wait_send()
    pltpu.make_async_remote_copy(
        src_ref=goff.at[other],
        dst_ref=goff.at[other],
        send_sem=new_send.at[chunks],
        recv_sem=new_recv.at[chunks],
        device_id=partner,
        device_id_type=MESH,
    ).wait_recv()


def write_out(*refs):
    sources, targets, sem = refs[:4], refs[4:8], refs[8]
    copies = [
        pltpu.make_async_copy(src, dst, sem.at[i])
        for i, (src, dst) in enumerate(zip(sources, targets))
    ]
    for copy in copies:
        copy.start()
    for copy in copies:
        copy.wait()


def solution(mesh):
    n_space, n_member = mesh.shape["space"], mesh.shape["member"]
    groups = n_member // CORES

    def body(
        start_temp,
        cotangent,
        conductivity,
        porosity,
        surface_temp,
        surface_offset,
        basal_flux,
        thickness,
        tile_len,
    ):
        layers, rows, across = conductivity.shape
        chunks = layers // CORES
        half = rows // CORES
        extra = layers + half
        f32 = jnp.float32
        whole = (layers, rows, across)
        plane = (rows, across)
        dma = pltpu.SemaphoreType.DMA

        def vmem(*shape):
            return pltpu.VMEM(shape, f32)

        hbm = pl.BlockSpec(memory_space=pltpu.HBM)
        cells = layers * rows * across
        heated, adj, new, goff = pl.pallas_call(
            lambda *refs: kernel(n_space, groups, *refs),
            out_shape=[pltpu.VMEM(s, f32) for s in (whole, whole, whole, plane)],
            in_specs=[pl.BlockSpec(memory_space=pltpu.SMEM)] + [hbm] * 8,
            out_specs=[pl.BlockSpec(memory_space=pltpu.VMEM)] * 4,
            scratch_shapes=[vmem(*whole)] * 4
            + [vmem(*plane)] * 5
            + [vmem(*whole)] * 4
            + [
                vmem(chunks, *plane),
                vmem(groups, chunks, *plane),
                vmem(2, 4, layers, across),
                vmem(2, 3, layers, across),
                vmem(2, 2, layers, across),
                vmem(CORES, extra, across),
                vmem(extra, across),
                vmem(groups, extra, across),
                vmem(*plane),
                dma((3, 8)),
                dma((2,)),
                dma((2,)),
                dma((chunks + 1,)),
                dma((chunks + 1,)),
                dma((max(groups - 1, 1), chunks + 1)),
                dma((groups, chunks + 1)),
                dma((chunks + 1,)),
                dma((chunks + 1,)),
            ],
            compiler_params=pltpu.CompilerParams(
                collective_id=0, has_side_effects=True, vmem_limit_bytes=48 * 1024 * 1024
            ),
            cost_estimate=pl.CostEstimate(
                flops=100 * cells, bytes_accessed=28 * cells, transcendentals=3 * cells
            ),
            name="heat_step",
        )(
            tile_len,
            *[
                pltpu.with_memory_space_constraint(x, pltpu.HBM)
                for x in (
                    start_temp[0],
                    porosity,
                    cotangent[0],
                    conductivity,
                    surface_temp[0],
                    surface_offset,
                    basal_flux,
                    thickness,
                )
            ]
        )
        heated, adj, new, goff = pl.pallas_call(
            write_out,
            out_shape=[pltpu.HBM(s, f32) for s in (whole, whole, whole, plane)],
            in_specs=[pl.BlockSpec(memory_space=pltpu.VMEM)] * 4,
            out_specs=[hbm] * 4,
            scratch_shapes=[dma((4,))],
            cost_estimate=pl.CostEstimate(flops=0, bytes_accessed=24 * cells, transcendentals=0),
            name="write_out",
        )(*[pltpu.with_memory_space_constraint(x, pltpu.VMEM) for x in (heated, adj, new, goff)])
        return heated[None], adj[None], new, goff

    in_specs = (
        P("member", None, "space", None),
        P("member", None, "space", None),
        P(None, "space", None),
        P(None, "space", None),
        P("member", "space", None),
        P("space", None),
        P("space", None),
        P("space", None),
        P("space"),
    )
    out_specs = (
        P("member", None, "space", None),
        P("member", None, "space", None),
        P(None, "space", None),
        P("space", None),
    )
    return jax.shard_map(body, mesh=mesh, in_specs=in_specs, out_specs=out_specs, check_vma=False)
```
